128 devices in a mesh: band: 32 (over y_hi, x, z), rep: 4 (over y_lo, core).
Axes of the slice: x: 4, y: 4 (y_hi: 2, y_lo: 2; y = y_hi * 2 + y_lo), z: 4, core: 2. Of those that a mesh axis runs over, the one named last changes fastest.
Arguments:
- feats: bfloat16 [524288, 128], P(('band', 'rep')), may hold values from -6 to 6
- tile_vals: bfloat16 [4096, 3, 128, 128], P(('band', 'rep')), may hold values from -0.3125 to 0.3125
- tile_offs: int32 [4096, 3], P(('band', 'rep')), may hold values from -16 to 16, as said below
- w_in: bfloat16 [2, 256, 128], replicated, may hold values from -0.375 to 0.375
- bias_in: float32 [2, 128], replicated, may hold values from -3 to 3
- w_out: bfloat16 [2, 128, 128], replicated, may hold values from -0.5 to 0.5
- gain: float32 [2, 128], replicated, may hold values from 0.1 to 1.9
- cot: bfloat16 [524288, 128], P(('band', 'rep')), may hold values from -6 to 6
Outputs:
- out_feats: bfloat16 [524288, 128], P(('band', 'rep'))
- grad_feats: float32 [524288, 128], P(('band', 'rep'))
- grad_w_in: float32 [2, 256, 128], replicated
- grad_bias_in: float32 [2, 128], replicated
- grad_w_out: float32 [2, 128, 128], replicated
- grad_gain: float32 [2, 128], replicated
The draws below stay inside these ranges and needn't reach their ends.
Inputs may be any that keep to these rules, and one draw needn't show every extreme that they name: `tile_offs`: in every block row slot 0 is 0, slot 1 lies in -16 to -1 and slot 2 in 1 to 16; block rows whose index is a multiple of 16 have -16 and 16.
All inputs are finite; a program needn't handle non-finite values.
Results may differ from the reference program's by a relative error of at most 0.0085.
Values may be sent and summed in bfloat16 or wider, within the bound.
A program may use at most 128 MiB of HBM per device.

```python
import math
import jax
import jax.numpy as jnp
from jax import lax

D = 128
HID = 128
BLK = 128
TPR = 3
HALO_BLK = 16
LAYERS = 2
NODES = 524288
BLOCKS = 4096
N_BAND = 32
N_REP = 4


def draw_tile_offs(key, part):
    key_low, key_high = jax.random.split(key)
    lower_off = -jax.random.randint(key_low, (BLOCKS,), 1, HALO_BLK + 1, dtype=jnp.int32)
    upper_off = jax.random.randint(key_high, (BLOCKS,), 1, HALO_BLK + 1, dtype=jnp.int32)
    marked = jnp.arange(BLOCKS, dtype=jnp.int32) % HALO_BLK == 0
    lower_off = jnp.where(marked, -HALO_BLK, lower_off)
    upper_off = jnp.where(marked, HALO_BLK, upper_off)
    return jnp.stack([jnp.zeros((BLOCKS,), jnp.int32), lower_off, upper_off], axis=1)


def levels(stream_key, extent, shards, low, top_value):
    def one(axis_at, shards_of):
        draws = jax.random.uniform(jax.random.fold_in(jax.random.fold_in(stream_key, 6), axis_at), (shards_of,), jnp.float32, low / len(shards), top_value / len(shards))
        return jnp.repeat(jnp.exp(draws), extent[axis_at] // shards_of).reshape((-1,) + (1,) * (len(extent) - axis_at - 1))

    level = one(*shards[0])
    for cut in shards[1:]:
        level = level * one(*cut)
    return level


def scatter_about(own_key, extent, spread, most, cuts=(), held_as=jnp.bfloat16):
    entries = spread * jax.random.normal(own_key, extent, jnp.float32)
    if cuts:
        entries = entries * levels(own_key, extent, cuts, -0.22, 0.18)
    return jnp.clip(entries, -most, most).astype(held_as)


def setup_inputs(seed: int = 0) -> dict:
    arg_keys = jax.random.split(jax.random.key(seed), 9)
    return {
        "feats": scatter_about(arg_keys[0], (NODES, D), 1.0, 6.0, ((0, 128),)),
        "tile_vals": scatter_about(arg_keys[1], (BLOCKS, TPR, BLK, BLK), (TPR * BLK) ** -0.5, 0.3125, ((0, 128),)),
        "tile_offs": draw_tile_offs(jax.random.fold_in(arg_keys[8], 71), 0),
        "w_in": scatter_about(arg_keys[3], (LAYERS, 2 * D, HID), (2 * D) ** -0.5, 0.375),
        "bias_in": scatter_about(arg_keys[4], (LAYERS, HID), 0.5, 3.0, (), jnp.float32),
        "w_out": scatter_about(arg_keys[5], (LAYERS, HID, D), HID ** -0.5, 0.5),
        "gain": jnp.clip(1.0 + 0.18 * jax.random.normal(arg_keys[6], (LAYERS, D), jnp.float32), 0.1, 1.9),
        "cot": scatter_about(arg_keys[7], (NODES, D), 1.0, 6.0, ((0, 128),)),
    }


def block_order(block_count):
    groups = N_BAND * N_REP
    return jnp.arange(block_count, dtype=jnp.int32).reshape(groups, block_count // groups)

def aggregate(feats_now, tile_vals, tile_offs):
    block_count = tile_vals.shape[0]
    tile_width = tile_vals.shape[2]
    feat_width = feats_now.shape[1]
    blocks = feats_now.reshape(block_count, tile_width, feat_width)

    def one_group(group_rows):
        columns = (group_rows[:, None] + tile_offs[group_rows]) % block_count
        pieces = blocks[columns].astype(jnp.float32)
        weights = tile_vals[group_rows].astype(jnp.float32)
        return jnp.einsum('bkij,bkjd->bid', weights, pieces).astype(jnp.bfloat16)
    result = lax.map(one_group, block_order(block_count))
    return result.reshape(-1, feat_width)

def spread_back(grad_agg, tile_vals, tile_offs):
    block_count = tile_vals.shape[0]
    tile_width = tile_vals.shape[2]
    feat_width = grad_agg.shape[1]
    grad_blocks = grad_agg.reshape(block_count, tile_width, feat_width)

    def add_group(running, group_rows):
        columns = (group_rows[:, None] + tile_offs[group_rows]) % block_count
        weights = tile_vals[group_rows].astype(jnp.float32)
        contrib = jnp.einsum('bkij,bid->bkjd', weights, grad_blocks[group_rows].astype(jnp.float32))
        running = running.at[columns.reshape(-1)].add(contrib.reshape(-1, tile_width, feat_width))
        return (running, None)
    initial = jnp.zeros((block_count, tile_width, feat_width), jnp.float32)
    running, unused = lax.scan(add_group, initial, block_order(block_count))
    return running.reshape(-1, feat_width)

def layer_forward(feats_now, agg_now, weight_in, bias_now, weight_out, gain_now):
    joined = jnp.concatenate([feats_now, agg_now], axis=1)
    pre_act = jnp.dot(joined, weight_in, preferred_element_type=jnp.float32) + bias_now
    act_now = jax.nn.silu(pre_act).astype(jnp.bfloat16)
    mixed = jnp.dot(act_now, weight_out, preferred_element_type=jnp.float32)
    centred = mixed - lax.optimization_barrier(jnp.mean(mixed, axis=1, keepdims=True))
    inv_std = lax.rsqrt(lax.optimization_barrier(jnp.mean(centred * centred, axis=1, keepdims=True)) + 1e-05)
    normed = centred * inv_std
    feats_next = (feats_now.astype(jnp.float32) + normed * gain_now).astype(jnp.bfloat16)
    return (feats_next, (joined, pre_act, act_now, normed, inv_std))

def layer_backward(grad_now, saved, weight_in, weight_out, gain_now):
    joined, pre_act, act_now, normed, inv_std = saved
    feat_width = gain_now.shape[0]
    grad_gain = lax.optimization_barrier(jnp.sum(grad_now * normed, axis=0))
    grad_norm = grad_now * gain_now
    grad_mix = inv_std * (grad_norm - lax.optimization_barrier(jnp.mean(grad_norm, axis=1, keepdims=True)) - normed * lax.optimization_barrier(jnp.mean(grad_norm * normed, axis=1, keepdims=True)))
    grad_mix_b = grad_mix.astype(jnp.bfloat16)
    grad_wout = lax.dot_general(act_now, grad_mix_b, (((0,), (0,)), ((), ())), preferred_element_type=jnp.float32)
    grad_act = lax.dot_general(grad_mix_b, weight_out, (((1,), (1,)), ((), ())), preferred_element_type=jnp.float32)
    sigma = jax.nn.sigmoid(pre_act)
    grad_pre = grad_act * sigma * (1.0 + pre_act * (1.0 - sigma))
    grad_bias = lax.optimization_barrier(jnp.sum(grad_pre, axis=0))
    grad_pre_b = grad_pre.astype(jnp.bfloat16)
    grad_win = lax.dot_general(joined, grad_pre_b, (((0,), (0,)), ((), ())), preferred_element_type=jnp.float32)
    grad_cat = lax.dot_general(grad_pre_b, weight_in, (((1,), (1,)), ((), ())), preferred_element_type=jnp.float32)
    grad_next = grad_now + grad_cat[:, :feat_width]
    grad_agg = grad_cat[:, feat_width:].astype(jnp.bfloat16)
    return (grad_next, grad_agg, grad_win, grad_bias, grad_wout, grad_gain)

def reference(feats, tile_vals, tile_offs, w_in, bias_in, w_out, gain, cot):
    feats_now = feats
    stored = []
    for layer_idx in range(LAYERS):
        agg_now = aggregate(feats_now, tile_vals, tile_offs)
        feats_now, saved = layer_forward(feats_now, agg_now, w_in[layer_idx], bias_in[layer_idx], w_out[layer_idx], gain[layer_idx])
        stored.append(saved)
    grad_now = cot.astype(jnp.float32)
    win_list, bias_list, wout_list, gain_list = ([], [], [], [])
    for layer_idx in reversed(range(LAYERS)):
        grad_now, grad_agg, grad_win, grad_bias, grad_wout, grad_gain = layer_backward(grad_now, stored[layer_idx], w_in[layer_idx], w_out[layer_idx], gain[layer_idx])
        grad_now = grad_now + spread_back(grad_agg, tile_vals, tile_offs)
        win_list.insert(0, grad_win)
        bias_list.insert(0, grad_bias)
        wout_list.insert(0, grad_wout)
        gain_list.insert(0, grad_gain)
    scale_factor = 1.0 / math.sqrt(NODES)
    return (feats_now, grad_now, jnp.stack(win_list) * scale_factor, jnp.stack(bias_list) * scale_factor, jnp.stack(wout_list) * scale_factor, jnp.stack(gain_list) * scale_factor)
```

```python
import functools
import math

import jax
import jax.numpy as jnp
from jax import lax
from jax.experimental import pallas as pl
from jax.experimental.pallas import tpu as pltpu
from jax.sharding import PartitionSpec as P

MESH = pl.DeviceIdType.MESH
HALO = 16
ROWS = 32
BLK = 128
CH = 4
NCH = HALO // CH
RB = 2
XZ = 16
LINE = 8
PIECE = 64
WROWS = 48
F32 = jnp.float32
BF16 = jnp.bfloat16

COL1, COL2 = 0, 32
PREV_A, PREV_B, PREV_C = 64, 80, 96
LAST_A, LAST_B, LAST_C = 128, 160, 192
TABLE = 224


def links_kernel(offs, tab):
    def clear(k, carry):
        tab[LAST_A + k] = -1
        return carry

    lax.fori_loop(0, 96, clear, 0)

    def low(i, carry):
        col = HALO + i + offs[i, 1]
        tab[COL1 + i] = col
        tab[PREV_A + i] = tab[LAST_A + col]
        tab[LAST_A + col] = i
        col = i + offs[i, 2]
        tab[COL2 + i] = HALO + col
        tab[PREV_C + i] = tab[LAST_C + col]
        tab[LAST_C + col] = i
        return carry

    lax.fori_loop(0, HALO, low, 0)

    def high(t, carry):
        i = ROWS - 1 - t
        col = i - HALO + offs[i, 2]
        tab[COL2 + i] = 2 * HALO + col
        tab[PREV_B + t] = tab[LAST_B + col]
        tab[LAST_B + col] = t
        col = i + offs[i, 1]
        tab[COL1 + i] = HALO + col
        tab[PREV_C + HALO + t] = tab[LAST_C + col]
        tab[LAST_C + col] = HALO + t
        return carry

    lax.fori_loop(0, HALO, high, 0)


def dot(a, b):
    return jnp.dot(a, b, preferred_element_type=F32)


def dot_nt(a, b):
    return lax.dot_general(a, b, (((1,), (1,)), ((), ())), preferred_element_type=F32)


def dot_tn(a, b):
    return lax.dot_general(a, b, (((0,), (0,)), ((), ())), preferred_element_type=F32)


def main_kernel(
    scale,
    feats, tiles_in, cot_in, tab, w_in, bias, w_out, gain,
    out_feats, grad_feats, out_win, out_bias, out_wout, out_gain,
    tiles, h0, h1, h2, cot, agg0, pre0, act0, xh0, inv0, gacc, gagg,
    seg_a, seg_b, seg_c, out_lo, out_hi, rx_lo, rx_hi, acc_w, acc_s,
    s1, r1, s2, r2, s3, r3,
    local_sem, store_sem, tx_lo_sem, tx_hi_sem, rx_lo_sem, rx_hi_sem,
    s1_sem, r1_sem, s2_sem, r2_sem, s3_sem, r3_sem,
):
    band, rep = lax.axis_index("band"), lax.axis_index("rep")
    n_rep, n_band = 4, 32
    me = band * n_rep + rep
    total = n_rep * n_band

    def place(index):
        return (lax.div(index, n_rep), lax.rem(index, n_rep))

    left = place(lax.rem(me + total - 1, total))
    right = place(lax.rem(me + 1, total))
    y_hi, plane = lax.div(band, XZ), lax.rem(band, XZ)
    line = y_hi * n_rep + rep

    def on_line(index):
        return (lax.div(index, n_rep) * XZ + plane, lax.rem(index, n_rep))

    def on_plane(index):
        return (y_hi * XZ + index, rep)

    barrier = pltpu.get_barrier_semaphore()
    for peer in (left, right):
        pl.semaphore_signal(barrier, inc=1, device_id=peer, device_id_type=MESH)
    for d in range(1, LINE):
        pl.semaphore_signal(barrier, inc=1, device_id=on_line(lax.rem(line + d, LINE)), device_id_type=MESH)
    for d in range(1, XZ):
        pl.semaphore_signal(barrier, inc=1, device_id=on_plane(lax.rem(plane + d, XZ)), device_id_type=MESH)

    get_feats = pltpu.make_async_copy(feats, h0.at[pl.ds(HALO, ROWS)], local_sem.at[0])
    get_tiles = pltpu.make_async_copy(tiles_in, tiles, local_sem.at[1])
    get_cot = pltpu.make_async_copy(cot_in, cot, local_sem.at[2])
    get_feats.start()
    get_tiles.start()
    get_cot.start()
    acc_w[...] = jnp.zeros_like(acc_w)
    acc_s[...] = jnp.zeros_like(acc_s)

    pl.semaphore_wait(barrier, 2 + LINE - 1 + XZ - 1)

    def to_left(x, c, src):
        return pltpu.make_async_remote_copy(
            src_ref=src, dst_ref=rx_hi.at[x, pl.ds(c * CH, CH)], send_sem=tx_lo_sem.at[x, c],
            recv_sem=rx_hi_sem.at[x, c], device_id=left, device_id_type=MESH,
        )

    def to_right(x, c, src):
        return pltpu.make_async_remote_copy(
            src_ref=src, dst_ref=rx_lo.at[x, pl.ds(c * CH, CH)], send_sem=tx_hi_sem.at[x, c],
            recv_sem=rx_lo_sem.at[x, c], device_id=right, device_id_type=MESH,
        )

    sent = []

    def go(copy):
        copy.start()
        sent.append(copy)
        return copy

    def wait_low(x, c):
        to_right(x, c, rx_lo.at[x, pl.ds(c * CH, CH)]).wait_recv()

    def wait_high(x, c):
        to_left(x, c, rx_hi.at[x, pl.ds(c * CH, CH)]).wait_recv()

    for s in range(NCH):
        c = NCH - 1 - s
        go(to_left(0, s, feats.at[pl.ds(s * CH, CH)]))
        go(to_right(0, c, feats.at[pl.ds(HALO + c * CH, CH)]))
    get_feats.wait()
    get_tiles.wait()

    def forward(layer, b, ext):
        own = ext[pl.ds(HALO + b, RB)]
        sums = []
        for r in range(RB):
            tile = tiles[b + r]
            lhs = jnp.concatenate([tile[0], tile[1]], axis=1)
            rhs = jnp.concatenate([own[r], ext[tab[COL1 + b + r]]], axis=0)
            sums.append((dot(lhs, rhs) + dot(tile[2], ext[tab[COL2 + b + r]])).astype(BF16))
        own = own.reshape(RB * BLK, BLK)
        agg = jnp.concatenate(sums, axis=0)
        cat = jnp.concatenate([own, agg], axis=1)
        pre = dot(cat, w_in[layer]) + bias[pl.ds(layer, 1), :]
        sig = 0.5 * jnp.tanh(0.5 * pre) + 0.5
        act = (pre * sig).astype(BF16)
        mix = dot(act, w_out[layer])
        cen = mix - jnp.mean(mix, axis=1, keepdims=True)
        inv = lax.rsqrt(jnp.mean(cen * cen, axis=1, keepdims=True) + 1e-05)
        xhat = cen * inv
        nxt = (own.astype(F32) + xhat * gain[pl.ds(layer, 1), :]).astype(BF16)
        return cat, agg, pre, sig, act, xhat, inv, nxt

    def backward(layer, b, g, cat, pre, sig, act, xhat, inv):
        gg = jnp.sum(g * xhat, axis=0, keepdims=True)
        gx = g * gain[pl.ds(layer, 1), :]
        gmix = inv * (
            gx - jnp.mean(gx, axis=1, keepdims=True) - xhat * jnp.mean(gx * xhat, axis=1, keepdims=True)
        )
        gmix_b = gmix.astype(BF16)
        gact = dot_nt(gmix_b, w_out[layer])
        gpre = gact * sig * (1.0 + pre * (1.0 - sig))
        gb = jnp.sum(gpre, axis=0, keepdims=True)
        gpre_b = gpre.astype(BF16)
        acc_w[layer, pl.ds(0, 256), :] += dot_tn(cat, gpre_b)
        acc_w[layer, pl.ds(256, 128), :] += dot_tn(act, gmix_b)
        acc_s[layer, pl.ds(0, 1), :] += gb
        acc_s[layer, pl.ds(1, 1), :] += gg
        gcat = dot_nt(gpre_b, w_in[layer])
        gacc[pl.ds(b, RB)] = (g + gcat[:, :BLK]).reshape(RB, BLK, BLK)
        gagg[pl.ds(b, RB)] = gcat[:, BLK:].astype(BF16).reshape(RB, BLK, BLK)

    def outward(s, k):
        per = CH // RB
        low = (NCH - 1 - s) * CH + k * RB
        high = HALO + s * CH + (k - per) * RB
        return jnp.where(k < per, low, high)

    def inward(s, k):
        per = CH // RB
        low = s * CH + k * RB
        high = (2 * NCH - 1 - s) * CH + (k - per) * RB
        return jnp.where(k < per, low, high)

    for s in range(NCH):
        c = NCH - 1 - s
        wait_low(0, c)
        wait_high(0, s)
        h0[pl.ds(c * CH, CH)] = rx_lo[0, pl.ds(c * CH, CH)]
        h0[pl.ds(HALO + ROWS + s * CH, CH)] = rx_hi[0, pl.ds(s * CH, CH)]

        def body0(k, carry, s=s):
            b = outward(s, k)
            cat, agg, pre, sig, act, xhat, inv, nxt = forward(0, b, h0)
            rows = pl.ds(b * BLK, RB * BLK)
            agg0[rows, :] = agg
            pre0[rows, :] = pre
            act0[rows, :] = act
            xh0[rows, :] = xhat
            inv0[rows, :] = inv
            h1[pl.ds(HALO + b, RB)] = nxt.reshape(RB, BLK, BLK)
            return carry

        lax.fori_loop(0, 2 * CH // RB, body0, 0)
        go(to_left(1, c, h1.at[pl.ds(HALO + c * CH, CH)]))
        go(to_right(1, s, h1.at[pl.ds(HALO + HALO + s * CH, CH)]))

    get_cot.wait()
    for s in range(NCH):
        c = NCH - 1 - s
        wait_low(1, c)
        wait_high(1, s)
        h1[pl.ds(c * CH, CH)] = rx_lo[1, pl.ds(c * CH, CH)]
        h1[pl.ds(HALO + ROWS + s * CH, CH)] = rx_hi[1, pl.ds(s * CH, CH)]

        def body1(k, carry, s=s):
            b = outward(s, k)
            cat, agg, pre, sig, act, xhat, inv, nxt = forward(1, b, h1)
            h2[pl.ds(b, RB)] = nxt.reshape(RB, BLK, BLK)
            g = cot[pl.ds(b, RB)].reshape(RB * BLK, BLK).astype(F32)
            backward(1, b, g, cat, pre, sig, act, xhat, inv)
            return carry

        lax.fori_loop(0, 2 * CH // RB, body1, 0)
    put_out = pltpu.make_async_copy(h2, out_feats, store_sem.at[0])
    put_out.start()

    def chain(seg, at, prev, value):
        seg[at] = value + jnp.where(prev >= 0, seg[jnp.maximum(prev, 0)], 0.0)

    def reach(s):
        def body(k, carry):
            t = s * CH + k
            chain(seg_a, t, tab[PREV_A + t], dot_tn(tiles[t, 1], gagg[t]))
            i = ROWS - 1 - t
            chain(seg_b, t, tab[PREV_B + t], dot_tn(tiles[i, 2], gagg[i]))
            return carry

        lax.fori_loop(0, CH, body, 0)

    def pick(seg, last):
        return jnp.where(last >= 0, seg[jnp.maximum(last, 0)], 0.0)

    def pack_low(y, c):
        def body(k, carry):
            out_lo[y, c * CH + k] = pick(seg_a, tab[LAST_A + c * CH + k]).astype(BF16)
            return carry

        lax.fori_loop(0, CH, body, 0)
        go(to_left(2 + y, c, out_lo.at[y, pl.ds(c * CH, CH)]))

    def pack_high(y, c):
        def body(k, carry):
            out_hi[y, c * CH + k] = pick(seg_b, tab[LAST_B + HALO + c * CH + k]).astype(BF16)
            return carry

        lax.fori_loop(0, CH, body, 0)
        go(to_right(2 + y, c, out_hi.at[y, pl.ds(c * CH, CH)]))

    def inside():
        def body(t, carry):
            chain(seg_c, t, tab[PREV_C + t], dot_tn(tiles[t, 2], gagg[t]))
            return carry

        lax.fori_loop(0, HALO, body, 0)

        def body2(t, carry):
            i = ROWS - 1 - t
            chain(seg_c, HALO + t, tab[PREV_C + HALO + t], dot_tn(tiles[i, 1], gagg[i]))
            return carry

        lax.fori_loop(0, HALO, body2, 0)

        def body3(j, carry):
            gacc[j] += (
                dot_tn(tiles[j, 0], gagg[j]) + pick(seg_c, tab[LAST_C + j]) + pick(seg_a, tab[LAST_A + HALO + j])
            )
            i = HALO + j
            gacc[i] += dot_tn(tiles[i, 0], gagg[i]) + pick(seg_c, tab[LAST_C + i]) + pick(seg_b, tab[LAST_B + j])
            return carry

        lax.fori_loop(0, HALO, body3, 0)

    def line_copy(layer, d):
        peer = lax.rem(line + d, LINE)
        return pltpu.make_async_remote_copy(
            src_ref=s1.at[layer, peer], dst_ref=r1.at[layer, d - 1], send_sem=s1_sem.at[layer, d - 1],
            recv_sem=r1_sem.at[layer, d - 1], device_id=on_line(peer), device_id_type=MESH,
        )

    def plane_copy(layer, d):
        return pltpu.make_async_remote_copy(
            src_ref=s2.at[layer], dst_ref=r2.at[layer, plane], send_sem=s2_sem.at[layer, d - 1],
            recv_sem=r2_sem.at[layer, d - 1], device_id=on_plane(lax.rem(plane + d, XZ)), device_id_type=MESH,
        )

    def gather_copy(layer, d):
        return pltpu.make_async_remote_copy(
            src_ref=s3.at[layer], dst_ref=r3.at[layer, line], send_sem=s3_sem.at[layer, d - 1],
            recv_sem=r3_sem.at[layer, d - 1], device_id=on_line(lax.rem(line + d, LINE)), device_id_type=MESH,
        )

    def reduce_line_start(layer):
        for p in range(LINE):
            s1[layer, p, pl.ds(0, WROWS), :] = acc_w[layer, pl.ds(p * WROWS, WROWS), :].astype(BF16)
            s1[layer, p, pl.ds(WROWS, 16), :] = acc_s[layer].astype(BF16)
        for d in range(1, LINE):
            line_copy(layer, d).start()

    def reduce_plane_start(layer):
        for d in range(1, LINE):
            line_copy(layer, d).wait()
        summed = s1[layer, line].astype(F32)
        for d in range(1, LINE):
            summed += r1[layer, d - 1].astype(F32)
        s2[layer] = summed.astype(BF16)
        r2[layer, plane] = summed.astype(BF16)
        for d in range(1, XZ):
            plane_copy(layer, d).start()

    def gather_start(layer):
        for d in range(1, XZ):
            plane_copy(layer, d).wait()
        summed = r2[layer, 0].astype(F32)
        for p in range(1, XZ):
            summed += r2[layer, p].astype(F32)
        s3[layer] = summed * scale
        r3[layer, line] = summed * scale
        for d in range(1, LINE):
            gather_copy(layer, d).start()

    def finish(layer):
        for d in range(1, LINE):
            gather_copy(layer, d).wait()
        for p in range(LINE):
            piece = r3[layer, p, pl.ds(0, WROWS), :]
            lo, hi = p * WROWS, (p + 1) * WROWS
            cut = min(max(256 - lo, 0), WROWS)
            if cut > 0:
                out_win[layer, pl.ds(lo, cut), :] = piece[:cut]
            if cut < WROWS:
                out_wout[layer, pl.ds(lo + cut - 256, WROWS - cut), :] = piece[cut:]
        out_bias[pl.ds(layer, 1), :] = r3[layer, 0, pl.ds(WROWS, 1), :]
        out_gain[pl.ds(layer, 1), :] = r3[layer, 0, pl.ds(WROWS + 1, 1), :]

    for s in range(NCH):
        reach(s)
    for s in range(NCH):
        pack_low(0, NCH - 1 - s)
        pack_high(0, s)
    reduce_line_start(1)
    inside()

    for s in range(NCH):
        c = NCH - 1 - s
        wait_low(2, s)
        wait_high(2, c)

        def body2(k, carry, s=s):
            b = inward(s, k)
            rows = pl.ds(b * BLK, RB * BLK)
            low = b < HALO
            at_lo = jnp.where(low, b, s * CH)
            at_hi = jnp.where(low, (NCH - 1 - s) * CH, b - HALO)
            come = jnp.where(low, rx_lo[2, pl.ds(at_lo, RB)], rx_hi[2, pl.ds(at_hi, RB)])
            g = (gacc[pl.ds(b, RB)] + come.astype(F32)).reshape(RB * BLK, BLK)
            cat = jnp.concatenate([h0[pl.ds(HALO + b, RB)].reshape(RB * BLK, BLK), agg0[rows, :]], axis=1)
            pre = pre0[rows, :]
            sig = 0.5 * jnp.tanh(0.5 * pre) + 0.5
            backward(0, b, g, cat, pre, sig, act0[rows, :], xh0[rows, :], inv0[rows, :])
            return carry

        lax.fori_loop(0, 2 * CH // RB, body2, 0)
        reach(s)
        pack_low(1, s)
        pack_high(1, c)
        if s == 0:
            reduce_plane_start(1)
        if s == 2:
            gather_start(1)
    reduce_line_start(0)
    inside()
    finish(1)
    reduce_plane_start(0)

    puts = []
    for s in range(NCH):
        c = NCH - 1 - s
        wait_low(3, c)
        wait_high(3, s)
        for b, rx, at in ((c * CH, rx_lo, c * CH), (HALO + s * CH, rx_hi, s * CH)):
            for k in range(CH):
                gacc[b + k] += rx[3, at + k].astype(F32)
            put = pltpu.make_async_copy(
                gacc.at[pl.ds(b, CH)], grad_feats.at[pl.ds(b, CH)], store_sem.at[1 + b // CH]
            )
            put.start()
            puts.append(put)
        if s == 2:
            gather_start(0)
    finish(0)
    put_out.wait()
    for put in puts:
        put.wait()
    for copy in sent:
        copy.wait_send()


def per_device(feats, tile_vals, tile_offs, w_in, bias_in, w_out, gain, cot):
    nodes, width = feats.shape
    total = nodes * lax.axis_size("band") * lax.axis_size("rep")
    scale = 1.0 / math.sqrt(total)
    smem = pl.BlockSpec(memory_space=pltpu.SMEM)
    vmem = pl.BlockSpec(memory_space=pltpu.VMEM)
    hbm = pl.BlockSpec(memory_space=pl.ANY)
    table = pl.pallas_call(
        links_kernel,
        out_shape=jax.ShapeDtypeStruct((TABLE,), jnp.int32),
        in_specs=[smem],
        out_specs=smem,
    )(tile_offs)

    blocks = (ROWS, BLK, width)
    ext = (ROWS + 2 * HALO, BLK, width)
    dma = pltpu.SemaphoreType.DMA
    outs = pl.pallas_call(
        functools.partial(main_kernel, scale),
        out_shape=(
            jax.ShapeDtypeStruct(blocks, BF16),
            jax.ShapeDtypeStruct(blocks, F32),
            jax.ShapeDtypeStruct(w_in.shape, F32),
            jax.ShapeDtypeStruct(bias_in.shape, F32),
            jax.ShapeDtypeStruct(w_out.shape, F32),
            jax.ShapeDtypeStruct(gain.shape, F32),
        ),
        in_specs=[hbm, hbm, hbm, smem, vmem, vmem, vmem, vmem],
        out_specs=(hbm, hbm, vmem, vmem, vmem, vmem),
        scratch_shapes=[
            pltpu.VMEM(tile_vals.shape, BF16),
            pltpu.VMEM(ext, BF16),
            pltpu.VMEM(ext, BF16),
            pltpu.VMEM(blocks, BF16),
            pltpu.VMEM(blocks, BF16),
            pltpu.VMEM((nodes, width), BF16),
            pltpu.VMEM((nodes, width), F32),
            pltpu.VMEM((nodes, width), BF16),
            pltpu.VMEM((nodes, width), F32),
            pltpu.VMEM((nodes, 1), F32),
            pltpu.VMEM(blocks, F32),
            pltpu.VMEM(blocks, BF16),
            pltpu.VMEM((HALO, BLK, width), F32),
            pltpu.VMEM((HALO, BLK, width), F32),
            pltpu.VMEM((ROWS, BLK, width), F32),
            pltpu.VMEM((2, HALO, BLK, width), BF16),
            pltpu.VMEM((2, HALO, BLK, width), BF16),
            pltpu.VMEM((4, HALO, BLK, width), BF16),
            pltpu.VMEM((4, HALO, BLK, width), BF16),
            pltpu.VMEM((2, 384, 128), F32),
            pltpu.VMEM((2, 16, 128), F32),
            pltpu.VMEM((2, LINE, PIECE, 128), BF16),
            pltpu.VMEM((2, LINE - 1, PIECE, 128), BF16),
            pltpu.VMEM((2, PIECE, 128), BF16),
            pltpu.VMEM((2, XZ, PIECE, 128), BF16),
            pltpu.VMEM((2, PIECE, 128), F32),
            pltpu.VMEM((2, LINE, PIECE, 128), F32),
            dma((3,)),
            dma((9,)),
            dma((4, NCH)),
            dma((4, NCH)),
            dma((4, NCH)),
            dma((4, NCH)),
            dma((2, LINE - 1)),
            dma((2, LINE - 1)),
            dma((2, XZ - 1)),
            dma((2, XZ - 1)),
            dma((2, LINE - 1)),
            dma((2, LINE - 1)),
        ],
        compiler_params=pltpu.CompilerParams(
            collective_id=0, has_side_effects=True, vmem_limit_bytes=56 * 2**20
        ),
        cost_estimate=pl.CostEstimate(flops=4 * 10**9, bytes_accessed=9 * 10**6, transcendentals=10**6),
    )(feats.reshape(blocks), tile_vals, cot.reshape(blocks), table, w_in, bias_in, w_out, gain)
    return (outs[0].reshape(feats.shape), outs[1].reshape(feats.shape), *outs[2:])


def solution(mesh):
    rows = P(("band", "rep"), None)
    placed = (rows, P(("band", "rep"), None, None, None), rows, P(), P(), P(), P(), rows)
    return jax.shard_map(
        per_device,
        mesh=mesh,
        in_specs=placed,
        out_specs=(rows, rows, P(), P(), P(), P()),
        check_vma=False,
    )
```

```python
import functools
import math

import jax
import jax.numpy as jnp
from jax import lax
from jax.experimental import pallas as pl
from jax.experimental.pallas import tpu as pltpu
from jax.sharding import PartitionSpec as P

MESH = pl.DeviceIdType.MESH
HALO = 16
ROWS = 32
BLK = 128
CH = 4
NCH = HALO // CH
EARLY = 1
RB = 4
XZ = 16
LINE = 8
PIECE = 64
WROWS = 48
F32 = jnp.float32
BF16 = jnp.bfloat16

PREV_A, PREV_B, PREV_C = 0, 16, 32
LAST_A, LAST_B, LAST_C = 64, 96, 128
COLS_A, COLS_B, COLS_C = 160, 176, 192
TABLE = 224


def links(offs, tab):
    def columns(t, carry):
        i = ROWS - 1 - t
        tab[COLS_A + t] = HALO + t + offs[1, t]
        tab[COLS_B + t] = i - HALO + offs[2, i]
        tab[COLS_C + t] = t + offs[2, t]
        tab[COLS_C + HALO + t] = i + offs[1, i]
        return carry

    lax.fori_loop(0, HALO, columns, 0)
    for cols, prev, last, count in (
        (COLS_A, PREV_A, LAST_A, HALO), (COLS_B, PREV_B, LAST_B, HALO), (COLS_C, PREV_C, LAST_C, 2 * HALO)
    ):
        def find_prev(e, carry, cols=cols, prev=prev, count=count):
            col, found = tab[cols + e], jnp.int32(-1)
            for k in range(count):
                found = jnp.where((tab[cols + k] == col) & (k < e), k, found)
            tab[prev + e] = found
            return carry

        def find_last(c, carry, cols=cols, last=last, count=count):
            found = jnp.int32(-1)
            for k in range(count):
                found = jnp.where(tab[cols + k] == c, k, found)
            tab[last + c] = found
            return carry

        lax.fori_loop(0, count, find_prev, 0)
        lax.fori_loop(0, ROWS, find_last, 0)


def dot(a, b):
    return jnp.dot(a, b, preferred_element_type=F32)


def dot_nt(a, b):
    return lax.dot_general(a, b, (((1,), (1,)), ((), ())), preferred_element_type=F32)


def dot_tn(a, b):
    return lax.dot_general(a, b, (((0,), (0,)), ((), ())), preferred_element_type=F32)


def main_kernel(
    scale,
    feats, tiles_in, cot_in, offs, w_in, bias, w_out, gain,
    h2, gacc, out_win, out_bias, out_wout, out_gain,
    tab, tiles, h0, h1, cot, agg0, pre0, act0, xh0, inv0, gagg,
    seg_a, seg_b, seg_c, out_lo, out_hi, rx_lo, rx_hi, acc_w, acc_s,
    s1, r1, s2, r2, s3, r3,
    local_sem, tx_lo_sem, tx_hi_sem, rx_lo_sem, rx_hi_sem,
    s1_sem, r1_sem, s2_sem, r2_sem, s3_sem, r3_sem,
):
    band, rep = lax.axis_index("band"), lax.axis_index("rep")
    n_rep, n_band = 4, 32
    me = band * n_rep + rep
    total = n_rep * n_band

    def place(index):
        return (lax.div(index, n_rep), lax.rem(index, n_rep))

    left = place(lax.rem(me + total - 1, total))
    right = place(lax.rem(me + 1, total))
    y_hi, x, z = lax.div(band, 16), lax.rem(lax.div(band, 4), 4), lax.rem(band, 4)
    y_lo, core = lax.div(rep, 2), lax.rem(rep, 2)
    line = x * 2 + core
    plane = z * 4 + y_hi * 2 + y_lo

    def on_line(index):
        return (y_hi * 16 + lax.div(index, 2) * 4 + z, y_lo * 2 + lax.rem(index, 2))

    def on_plane(index):
        return (
            lax.rem(lax.div(index, 2), 2) * 16 + x * 4 + lax.div(index, 4),
            lax.rem(index, 2) * 2 + core,
        )

    barrier = pltpu.get_barrier_semaphore()
    for peer in (left, right):
        pl.semaphore_signal(barrier, inc=1, device_id=peer, device_id_type=MESH)
    for d in range(1, LINE):
        pl.semaphore_signal(barrier, inc=1, device_id=on_line(lax.rem(line + d, LINE)), device_id_type=MESH)
    for d in range(1, XZ):
        pl.semaphore_signal(barrier, inc=1, device_id=on_plane(lax.rem(plane + d, XZ)), device_id_type=MESH)

    get_feats = pltpu.make_async_copy(feats, h0.at[pl.ds(HALO, ROWS)], local_sem.at[0])
    get_tiles = pltpu.make_async_copy(tiles_in, tiles, local_sem.at[1])
    get_cot = pltpu.make_async_copy(cot_in, cot, local_sem.at[2])
    get_feats.start()
    get_tiles.start()
    get_cot.start()
    acc_w[...] = jnp.zeros_like(acc_w)
    acc_s[...] = jnp.zeros_like(acc_s)

    pl.semaphore_wait(barrier, 2 + LINE - 1 + XZ - 1)

    def to_left(x, c, src):
        return pltpu.make_async_remote_copy(
            src_ref=src, dst_ref=rx_hi.at[x, pl.ds(c * CH, CH)], send_sem=tx_lo_sem.at[x, c],
            recv_sem=rx_hi_sem.at[x, c], device_id=left, device_id_type=MESH,
        )

    def to_right(x, c, src):
        return pltpu.make_async_remote_copy(
            src_ref=src, dst_ref=rx_lo.at[x, pl.ds(c * CH, CH)], send_sem=tx_hi_sem.at[x, c],
            recv_sem=rx_lo_sem.at[x, c], device_id=right, device_id_type=MESH,
        )

    sent = []

    def go(copy):
        copy.start()
        sent.append(copy)
        return copy

    def wait_low(x, c):
        to_right(x, c, rx_lo.at[x, pl.ds(c * CH, CH)]).wait_recv()

    def wait_high(x, c):
        to_left(x, c, rx_hi.at[x, pl.ds(c * CH, CH)]).wait_recv()

    for s in range(NCH):
        c = NCH - 1 - s
        go(to_left(0, s, feats.at[pl.ds(s * CH, CH)]))
        go(to_right(0, c, feats.at[pl.ds(HALO + c * CH, CH)]))
    links(offs, tab)
    get_feats.wait()
    get_tiles.wait()

    def forward(layer, b, ext):
        own = ext[pl.ds(HALO + b, RB)]
        sums = []
        for r in range(RB):
            tile = tiles[b + r]
            lhs = jnp.concatenate([tile[0], tile[1]], axis=1)
            rhs = jnp.concatenate([own[r], ext[HALO + b + r + offs[1, b + r]]], axis=0)
            sums.append((dot(lhs, rhs) + dot(tile[2], ext[HALO + b + r + offs[2, b + r]])).astype(BF16))
        own = own.reshape(RB * BLK, BLK)
        agg = jnp.concatenate(sums, axis=0)
        cat = jnp.concatenate([own, agg], axis=1)
        pre = dot(cat, w_in[layer]) + bias[pl.ds(layer, 1), :]
        sig = 0.5 * jnp.tanh(0.5 * pre) + 0.5
        act = (pre * sig).astype(BF16)
        mix = dot(act, w_out[layer])
        cen = mix - jnp.mean(mix, axis=1, keepdims=True)
        inv = lax.rsqrt(jnp.mean(cen * cen, axis=1, keepdims=True) + 1e-05)
        xhat = cen * inv
        nxt = (own.astype(F32) + xhat * gain[pl.ds(layer, 1), :]).astype(BF16)
        return cat, agg, pre, sig, act, xhat, inv, nxt

    def backward(layer, b, g, cat, pre, sig, act, xhat, inv):
        gg = jnp.sum(g * xhat, axis=0, keepdims=True)
        gx = g * gain[pl.ds(layer, 1), :]
        gmix = inv * (
            gx - jnp.mean(gx, axis=1, keepdims=True) - xhat * jnp.mean(gx * xhat, axis=1, keepdims=True)
        )
        gmix_b = gmix.astype(BF16)
        gact = dot_nt(gmix_b, w_out[layer])
        gpre = gact * sig * (1.0 + pre * (1.0 - sig))
        gb = jnp.sum(gpre, axis=0, keepdims=True)
        gpre_b = gpre.astype(BF16)
        acc_w[layer, pl.ds(0, 256), :] += dot_tn(cat, gpre_b)
        acc_w[layer, pl.ds(256, 128), :] += dot_tn(act, gmix_b)
        acc_s[layer, pl.ds(0, 1), :] += gb
        acc_s[layer, pl.ds(1, 1), :] += gg
        gcat = dot_nt(gpre_b, w_in[layer])
        gacc[pl.ds(b, RB)] = (g + gcat[:, :BLK]).reshape(RB, BLK, BLK)
        gagg[pl.ds(b, RB)] = gcat[:, BLK:].astype(BF16).reshape(RB, BLK, BLK)

    def outward(s, k):
        per = CH // RB
        low = (NCH - 1 - s) * CH + k * RB
        high = HALO + s * CH + (k - per) * RB
        return jnp.where(k < per, low, high)

    def inward(s, k):
        per = CH // RB
        low = s * CH + k * RB
        high = (2 * NCH - 1 - s) * CH + (k - per) * RB
        return jnp.where(k < per, low, high)

    for s in range(NCH):
        c = NCH - 1 - s
        wait_low(0, c)
        wait_high(0, s)
        h0[pl.ds(c * CH, CH)] = rx_lo[0, pl.ds(c * CH, CH)]
        h0[pl.ds(HALO + ROWS + s * CH, CH)] = rx_hi[0, pl.ds(s * CH, CH)]

        def body0(k, carry, s=s):
            b = outward(s, k)
            cat, agg, pre, sig, act, xhat, inv, nxt = forward(0, b, h0)
            rows = pl.ds(b * BLK, RB * BLK)
            agg0[rows, :] = agg
            pre0[rows, :] = pre
            act0[rows, :] = act
            xh0[rows, :] = xhat
            inv0[rows, :] = inv
            h1[pl.ds(HALO + b, RB)] = nxt.reshape(RB, BLK, BLK)
            return carry

        lax.fori_loop(0, 2 * CH // RB, body0, 0, unroll=2)
        for late in (s,) if s < EARLY else range(NCH - 1, EARLY - 1, -1) if s == NCH - 1 else ():
            c = NCH - 1 - late
            go(to_left(1, c, h1.at[pl.ds(HALO + c * CH, CH)]))
            go(to_right(1, late, h1.at[pl.ds(HALO + HALO + late * CH, CH)]))

    get_cot.wait()
    for s in range(NCH):
        c = NCH - 1 - s
        wait_low(1, c)
        wait_high(1, s)
        h1[pl.ds(c * CH, CH)] = rx_lo[1, pl.ds(c * CH, CH)]
        h1[pl.ds(HALO + ROWS + s * CH, CH)] = rx_hi[1, pl.ds(s * CH, CH)]

        def body1(k, carry, s=s):
            b = outward(s, k)
            cat, agg, pre, sig, act, xhat, inv, nxt = forward(1, b, h1)
            h2[pl.ds(b, RB)] = nxt.reshape(RB, BLK, BLK)
            g = cot[pl.ds(b, RB)].reshape(RB * BLK, BLK).astype(F32)
            backward(1, b, g, cat, pre, sig, act, xhat, inv)
            return carry

        lax.fori_loop(0, 2 * CH // RB, body1, 0, unroll=2)

    def chain(seg, at, prev, value):
        seg[at] = value + jnp.where(prev >= 0, seg[jnp.maximum(prev, 0)], 0.0)

    def reach(s):
        def body(k, carry):
            t = s * CH + k
            chain(seg_a, t, tab[PREV_A + t], dot_tn(tiles[t, 1], gagg[t]))
            i = ROWS - 1 - t
            chain(seg_b, t, tab[PREV_B + t], dot_tn(tiles[i, 2], gagg[i]))
            return carry

        lax.fori_loop(0, CH, body, 0, unroll=4)

    def pick(seg, last):
        return jnp.where(last >= 0, seg[jnp.maximum(last, 0)], 0.0)

    def pack_low(y, c):
        def body(k, carry):
            out_lo[y, c * CH + k] = pick(seg_a, tab[LAST_A + c * CH + k]).astype(BF16)
            return carry

        lax.fori_loop(0, CH, body, 0, unroll=4)
        go(to_left(2 + y, c, out_lo.at[y, pl.ds(c * CH, CH)]))

    def pack_high(y, c):
        def body(k, carry):
            out_hi[y, c * CH + k] = pick(seg_b, tab[LAST_B + HALO + c * CH + k]).astype(BF16)
            return carry

        lax.fori_loop(0, CH, body, 0, unroll=4)
        go(to_right(2 + y, c, out_hi.at[y, pl.ds(c * CH, CH)]))

    def inside():
        def body(t, carry):
            chain(seg_c, t, tab[PREV_C + t], dot_tn(tiles[t, 2], gagg[t]))
            return carry

        lax.fori_loop(0, HALO, body, 0, unroll=16)

        def body2(t, carry):
            i = ROWS - 1 - t
            chain(seg_c, HALO + t, tab[PREV_C + HALO + t], dot_tn(tiles[i, 1], gagg[i]))
            return carry

        lax.fori_loop(0, HALO, body2, 0, unroll=16)

        def body3(j, carry):
            gacc[j] += (
                dot_tn(tiles[j, 0], gagg[j]) + pick(seg_c, tab[LAST_C + j]) + pick(seg_a, tab[LAST_A + HALO + j])
            )
            i = HALO + j
            gacc[i] += dot_tn(tiles[i, 0], gagg[i]) + pick(seg_c, tab[LAST_C + i]) + pick(seg_b, tab[LAST_B + j])
            return carry

        lax.fori_loop(0, HALO, body3, 0, unroll=16)

    def line_copy(layer, d):
        peer = lax.rem(line + d, LINE)
        return pltpu.make_async_remote_copy(
            src_ref=s1.at[layer, peer], dst_ref=r1.at[layer, d - 1], send_sem=s1_sem.at[layer, d - 1],
            recv_sem=r1_sem.at[layer, d - 1], device_id=on_line(peer), device_id_type=MESH,
        )

    def plane_copy(layer, d):
        return pltpu.make_async_remote_copy(
            src_ref=s2.at[layer], dst_ref=r2.at[layer, plane], send_sem=s2_sem.at[layer, d - 1],
            recv_sem=r2_sem.at[layer, d - 1], device_id=on_plane(lax.rem(plane + d, XZ)), device_id_type=MESH,
        )

    def gather_copy(layer, d):
        return pltpu.make_async_remote_copy(
            src_ref=s3.at[layer], dst_ref=r3.at[layer, line], send_sem=s3_sem.at[layer, d - 1],
            recv_sem=r3_sem.at[layer, d - 1], device_id=on_line(lax.rem(line + d, LINE)), device_id_type=MESH,
        )

    def reduce_line_start(layer):
        for p in range(LINE):
            s1[layer, p, pl.ds(0, WROWS), :] = acc_w[layer, pl.ds(p * WROWS, WROWS), :].astype(BF16)
            s1[layer, p, pl.ds(WROWS, 16), :] = acc_s[layer].astype(BF16)
        for d in range(1, LINE):
            line_copy(layer, d).start()

    def reduce_plane_start(layer):
        for d in range(1, LINE):
            line_copy(layer, d).wait()
        summed = s1[layer, line].astype(F32)
        for d in range(1, LINE):
            summed += r1[layer, d - 1].astype(F32)
        s2[layer] = summed.astype(BF16)
        r2[layer, plane] = summed.astype(BF16)
        for d in range(1, XZ):
            plane_copy(layer, d).start()

    def gather_start(layer):
        for d in range(1, XZ):
            plane_copy(layer, d).wait()
        summed = r2[layer, 0].astype(F32)
        for p in range(1, XZ):
            summed += r2[layer, p].astype(F32)
        s3[layer] = summed * scale
        r3[layer, line] = summed * scale
        for d in range(1, LINE):
            gather_copy(layer, d).start()

    def finish(layer):
        for d in range(1, LINE):
            gather_copy(layer, d).wait()
        for p in range(LINE):
            piece = r3[layer, p, pl.ds(0, WROWS), :]
            lo, hi = p * WROWS, (p + 1) * WROWS
            cut = min(max(256 - lo, 0), WROWS)
            if cut > 0:
                out_win[layer, pl.ds(lo, cut), :] = piece[:cut]
            if cut < WROWS:
                out_wout[layer, pl.ds(lo + cut - 256, WROWS - cut), :] = piece[cut:]
        out_bias[pl.ds(layer, 1), :] = r3[layer, 0, pl.ds(WROWS, 1), :]
        out_gain[pl.ds(layer, 1), :] = r3[layer, 0, pl.ds(WROWS + 1, 1), :]

    for s in range(NCH):
        reach(s)
    for s in range(NCH):
        pack_low(0, NCH - 1 - s)
        pack_high(0, s)
    reduce_line_start(1)
    inside()

    for s in range(NCH):
        c = NCH - 1 - s
        wait_low(2, s)
        wait_high(2, c)

        def body2(k, carry, s=s):
            b = inward(s, k)
            rows = pl.ds(b * BLK, RB * BLK)
            low = b < HALO
            at_lo = jnp.where(low, b, s * CH)
            at_hi = jnp.where(low, (NCH - 1 - s) * CH, b - HALO)
            come = jnp.where(low, rx_lo[2, pl.ds(at_lo, RB)], rx_hi[2, pl.ds(at_hi, RB)])
            g = (gacc[pl.ds(b, RB)] + come.astype(F32)).reshape(RB * BLK, BLK)
            cat = jnp.concatenate([h0[pl.ds(HALO + b, RB)].reshape(RB * BLK, BLK), agg0[rows, :]], axis=1)
            pre = pre0[rows, :]
            sig = 0.5 * jnp.tanh(0.5 * pre) + 0.5
            backward(0, b, g, cat, pre, sig, act0[rows, :], xh0[rows, :], inv0[rows, :])
            return carry

        lax.fori_loop(0, 2 * CH // RB, body2, 0, unroll=2)
        reach(s)
        pack_low(1, s)
        pack_high(1, c)
        if s == 0:
            reduce_plane_start(1)
        if s == 2:
            gather_start(1)
    reduce_line_start(0)
    inside()
    finish(1)
    reduce_plane_start(0)

    for s in range(NCH):
        c = NCH - 1 - s
        wait_low(3, c)
        wait_high(3, s)
        for b, rx, at in ((c * CH, rx_lo, c * CH), (HALO + s * CH, rx_hi, s * CH)):
            for k in range(CH):
                gacc[b + k] += rx[3, at + k].astype(F32)
        if s == 2:
            gather_start(0)
    finish(0)
    for copy in sent:
        copy.wait_send()


def publish_kernel(*refs):
    sem = refs[12]
    copies = [pltpu.make_async_copy(refs[k], refs[6 + k], sem.at[k]) for k in range(6)]
    for copy in copies:
        copy.start()
    for copy in copies:
        copy.wait()


def per_device(feats, tile_vals, tile_offs, w_in, bias_in, w_out, gain, cot):
    nodes, width = feats.shape
    total = nodes * lax.axis_size("band") * lax.axis_size("rep")
    scale = 1.0 / math.sqrt(total)
    smem = pl.BlockSpec(memory_space=pltpu.SMEM)
    vmem = pl.BlockSpec(memory_space=pltpu.VMEM)
    hbm = pl.BlockSpec(memory_space=pl.ANY)
    blocks = (ROWS, BLK, width)
    ext = (ROWS + 2 * HALO, BLK, width)
    dma = pltpu.SemaphoreType.DMA
    outs = pl.pallas_call(
        functools.partial(main_kernel, scale),
        out_shape=(
            pltpu.VMEM(blocks, BF16),
            pltpu.VMEM(blocks, F32),
            pltpu.VMEM(w_in.shape, F32),
            pltpu.VMEM(bias_in.shape, F32),
            pltpu.VMEM(w_out.shape, F32),
            pltpu.VMEM(gain.shape, F32),
        ),
        in_specs=[hbm, hbm, hbm, smem, vmem, vmem, vmem, vmem],
        out_specs=(vmem,) * 6,
        scratch_shapes=[
            pltpu.SMEM((TABLE,), jnp.int32),
            pltpu.VMEM(tile_vals.shape, BF16),
            pltpu.VMEM(ext, BF16),
            pltpu.VMEM(ext, BF16),
            pltpu.VMEM(blocks, BF16),
            pltpu.VMEM((nodes, width), BF16),
            pltpu.VMEM((nodes, width), F32),
            pltpu.VMEM((nodes, width), BF16),
            pltpu.VMEM((nodes, width), F32),
            pltpu.VMEM((nodes, 1), F32),
            pltpu.VMEM(blocks, BF16),
            pltpu.VMEM((HALO, BLK, width), F32),
            pltpu.VMEM((HALO, BLK, width), F32),
            pltpu.VMEM((ROWS, BLK, width), F32),
            pltpu.VMEM((2, HALO, BLK, width), BF16),
            pltpu.VMEM((2, HALO, BLK, width), BF16),
            pltpu.VMEM((4, HALO, BLK, width), BF16),
            pltpu.VMEM((4, HALO, BLK, width), BF16),
            pltpu.VMEM((2, 384, 128), F32),
            pltpu.VMEM((2, 16, 128), F32),
            pltpu.VMEM((2, LINE, PIECE, 128), BF16),
            pltpu.VMEM((2, LINE - 1, PIECE, 128), BF16),
            pltpu.VMEM((2, PIECE, 128), BF16),
            pltpu.VMEM((2, XZ, PIECE, 128), BF16),
            pltpu.VMEM((2, PIECE, 128), F32),
            pltpu.VMEM((2, LINE, PIECE, 128), F32),
            dma((3,)),
            dma((4, NCH)),
            dma((4, NCH)),
            dma((4, NCH)),
            dma((4, NCH)),
            dma((2, LINE - 1)),
            dma((2, LINE - 1)),
            dma((2, XZ - 1)),
            dma((2, XZ - 1)),
            dma((2, LINE - 1)),
            dma((2, LINE - 1)),
        ],
        compiler_params=pltpu.CompilerParams(
            collective_id=0, has_side_effects=True, vmem_limit_bytes=56 * 2**20
        ),
        cost_estimate=pl.CostEstimate(flops=4 * 10**9, bytes_accessed=9 * 10**6, transcendentals=10**6),
    )(feats.reshape(blocks), tile_vals, cot.reshape(blocks), tile_offs.T, w_in, bias_in, w_out, gain)
    outs = (outs[0].reshape(feats.shape), outs[1].reshape(feats.shape), *outs[2:])
    return pl.pallas_call(
        publish_kernel,
        out_shape=tuple(jax.ShapeDtypeStruct(o.shape, o.dtype) for o in outs),
        in_specs=[hbm] * 6,
        out_specs=(hbm,) * 6,
        scratch_shapes=[dma((6,))],
        compiler_params=pltpu.CompilerParams(vmem_limit_bytes=2**20),
    )(*outs)


def solution(mesh):
    rows = P(("band", "rep"), None)
    placed = (rows, P(("band", "rep"), None, None, None), rows, P(), P(), P(), P(), rows)
    return jax.shard_map(
        per_device,
        mesh=mesh,
        in_specs=placed,
        out_specs=(rows, rows, P(), P(), P(), P()),
        check_vma=False,
    )
```

```python
import functools
import math

import jax
import jax.numpy as jnp
from jax import lax
from jax.experimental import pallas as pl
from jax.experimental.pallas import tpu as pltpu
from jax.sharding import PartitionSpec as P

MESH = pl.DeviceIdType.MESH
HALO = 16
ROWS = 32
BLK = 128
CH = 4
NCH = HALO // CH
EARLY = 1
EARLY_BACK = 0
RB = 4
XZ = 16
LINE = 8
PIECE = 64
WROWS = 48
F32 = jnp.float32
BF16 = jnp.bfloat16

PREV_A, PREV_B, PREV_C = 0, 16, 32
LAST_A, LAST_B, LAST_C = 64, 96, 128
COLS_A, COLS_B, COLS_C = 160, 176, 192
TABLE = 224


def links(offs, tab):
    def columns(t, carry):
        i = ROWS - 1 - t
        tab[COLS_A + t] = HALO + t + offs[1, t]
        tab[COLS_B + t] = i - HALO + offs[2, i]
        tab[COLS_C + t] = t + offs[2, t]
        tab[COLS_C + HALO + t] = i + offs[1, i]
        return carry

    lax.fori_loop(0, HALO, columns, 0)
    for cols, prev, last, count in (
        (COLS_A, PREV_A, LAST_A, HALO), (COLS_B, PREV_B, LAST_B, HALO), (COLS_C, PREV_C, LAST_C, 2 * HALO)
    ):
        def find_prev(e, carry, cols=cols, prev=prev, count=count):
            col, found = tab[cols + e], jnp.int32(-1)
            for k in range(count):
                found = jnp.where((tab[cols + k] == col) & (k < e), k, found)
            tab[prev + e] = found
            return carry

        def find_last(c, carry, cols=cols, last=last, count=count):
            found = jnp.int32(-1)
            for k in range(count):
                found = jnp.where(tab[cols + k] == c, k, found)
            tab[last + c] = found
            return carry

        lax.fori_loop(0, count, find_prev, 0)
        lax.fori_loop(0, ROWS, find_last, 0)


def dot(a, b):
    return jnp.dot(a, b, preferred_element_type=F32)


def dot_nt(a, b):
    return lax.dot_general(a, b, (((1,), (1,)), ((), ())), preferred_element_type=F32)


def dot_tn(a, b):
    return lax.dot_general(a, b, (((0,), (0,)), ((), ())), preferred_element_type=F32)


def main_kernel(
    scale,
    feats, tiles_in, cot_in, offs, w_in, bias, w_out, gain,
    h2, gacc, out_win, out_bias, out_wout, out_gain,
    tab, tiles, h0, h1, cot, agg0, pre0, act0, xh0, inv0, gagg,
    seg_a, seg_b, seg_c, out_lo, out_hi, rx_lo, rx_hi, acc_w, acc_s,
    s1, r1, s2, r2, s3, r3,
    local_sem, tx_lo_sem, tx_hi_sem, rx_lo_sem, rx_hi_sem,
    s1_sem, r1_sem, s2_sem, r2_sem, s3_sem, r3_sem,
):
    band, rep = lax.axis_index("band"), lax.axis_index("rep")
    n_rep, n_band = 4, 32
    me = band * n_rep + rep
    total = n_rep * n_band

    def place(index):
        return (lax.div(index, n_rep), lax.rem(index, n_rep))

    left = place(lax.rem(me + total - 1, total))
    right = place(lax.rem(me + 1, total))
    y_hi, x, z = lax.div(band, 16), lax.rem(lax.div(band, 4), 4), lax.rem(band, 4)
    y_lo, core = lax.div(rep, 2), lax.rem(rep, 2)
    line = x * 2 + core
    plane = z * 4 + y_hi * 2 + y_lo

    def on_line(index):
        return (y_hi * 16 + lax.div(index, 2) * 4 + z, y_lo * 2 + lax.rem(index, 2))

    def on_plane(index):
        return (
            lax.rem(lax.div(index, 2), 2) * 16 + x * 4 + lax.div(index, 4),
            lax.rem(index, 2) * 2 + core,
        )

    barrier = pltpu.get_barrier_semaphore()
    for peer in (left, right):
        pl.semaphore_signal(barrier, inc=1, device_id=peer, device_id_type=MESH)
    for d in range(1, LINE):
        pl.semaphore_signal(barrier, inc=1, device_id=on_line(lax.rem(line + d, LINE)), device_id_type=MESH)
    for d in range(1, XZ):
        pl.semaphore_signal(barrier, inc=1, device_id=on_plane(lax.rem(plane + d, XZ)), device_id_type=MESH)

    get_feats = pltpu.make_async_copy(feats, h0.at[pl.ds(HALO, ROWS)], local_sem.at[0])
    get_tiles = pltpu.make_async_copy(tiles_in, tiles, local_sem.at[1])
    get_cot = pltpu.make_async_copy(cot_in, cot, local_sem.at[2])
    get_feats.start()
    get_tiles.start()
    get_cot.start()
    acc_w[...] = jnp.zeros_like(acc_w)
    acc_s[...] = jnp.zeros_like(acc_s)

    pl.semaphore_wait(barrier, 2 + LINE - 1 + XZ - 1)

    def to_left(x, c, src):
        return pltpu.make_async_remote_copy(
            src_ref=src, dst_ref=rx_hi.at[x, pl.ds(c * CH, CH)], send_sem=tx_lo_sem.at[x, c],
            recv_sem=rx_hi_sem.at[x, c], device_id=left, device_id_type=MESH,
        )

    def to_right(x, c, src):
        return pltpu.make_async_remote_copy(
            src_ref=src, dst_ref=rx_lo.at[x, pl.ds(c * CH, CH)], send_sem=tx_hi_sem.at[x, c],
            recv_sem=rx_lo_sem.at[x, c], device_id=right, device_id_type=MESH,
        )

    sent = []

    def go(copy):
        copy.start()
        sent.append(copy)
        return copy

    held = []

    def hold(copy):
        held.append(copy)

    def release(before=()):
        for copy in before:
            copy.wait_send()
            sent[:] = [k for k in sent if k is not copy]
        for copy in (held.pop(0), held.pop(0)):
            go(copy)
        return tuple(sent[-2:])

    def wait_low(x, c):
        to_right(x, c, rx_lo.at[x, pl.ds(c * CH, CH)]).wait_recv()

    def wait_high(x, c):
        to_left(x, c, rx_hi.at[x, pl.ds(c * CH, CH)]).wait_recv()

    for s in range(NCH):
        c = NCH - 1 - s
        go(to_left(0, s, feats.at[pl.ds(s * CH, CH)]))
        go(to_right(0, c, feats.at[pl.ds(HALO + c * CH, CH)]))
    links(offs, tab)
    get_feats.wait()
    get_tiles.wait()

    def forward(layer, b, ext):
        own = ext[pl.ds(HALO + b, RB)]
        sums = []
        for r in range(RB):
            tile = tiles[b + r]
            lhs = jnp.concatenate([tile[0], tile[1]], axis=1)
            rhs = jnp.concatenate([own[r], ext[HALO + b + r + offs[1, b + r]]], axis=0)
            sums.append((dot(lhs, rhs) + dot(tile[2], ext[HALO + b + r + offs[2, b + r]])).astype(BF16))
        own = own.reshape(RB * BLK, BLK)
        agg = jnp.concatenate(sums, axis=0)
        cat = jnp.concatenate([own, agg], axis=1)
        pre = dot(cat, w_in[layer]) + bias[pl.ds(layer, 1), :]
        sig = 0.5 * jnp.tanh(0.5 * pre) + 0.5
        act = (pre * sig).astype(BF16)
        mix = dot(act, w_out[layer])
        cen = mix - jnp.mean(mix, axis=1, keepdims=True)
        inv = lax.rsqrt(jnp.mean(cen * cen, axis=1, keepdims=True) + 1e-05)
        xhat = cen * inv
        nxt = (own.astype(F32) + xhat * gain[pl.ds(layer, 1), :]).astype(BF16)
        return cat, agg, pre, sig, act, xhat, inv, nxt

    def backward(layer, b, g, cat, pre, sig, act, xhat, inv):
        gg = jnp.sum(g * xhat, axis=0, keepdims=True)
        gx = g * gain[pl.ds(layer, 1), :]
        gmix = inv * (
            gx - jnp.mean(gx, axis=1, keepdims=True) - xhat * jnp.mean(gx * xhat, axis=1, keepdims=True)
        )
        gmix_b = gmix.astype(BF16)
        gact = dot_nt(gmix_b, w_out[layer])
        gpre = gact * sig * (1.0 + pre * (1.0 - sig))
        gb = jnp.sum(gpre, axis=0, keepdims=True)
        gpre_b = gpre.astype(BF16)
        acc_w[layer, pl.ds(0, 256), :] += dot_tn(cat, gpre_b)
        acc_w[layer, pl.ds(256, 128), :] += dot_tn(act, gmix_b)
        acc_s[layer, pl.ds(0, 1), :] += gb
        acc_s[layer, pl.ds(1, 1), :] += gg
        gcat = dot_nt(gpre_b, w_in[layer])
        gacc[pl.ds(b, RB)] = (g + gcat[:, :BLK]).reshape(RB, BLK, BLK)
        gagg[pl.ds(b, RB)] = gcat[:, BLK:].astype(BF16).reshape(RB, BLK, BLK)

    def outward(s, k):
        per = CH // RB
        low = (NCH - 1 - s) * CH + k * RB
        high = HALO + s * CH + (k - per) * RB
        return jnp.where(k < per, low, high)

    def inward(s, k):
        per = CH // RB
        low = s * CH + k * RB
        high = (2 * NCH - 1 - s) * CH + (k - per) * RB
        return jnp.where(k < per, low, high)

    for s in range(NCH):
        c = NCH - 1 - s
        wait_low(0, c)
        wait_high(0, s)
        h0[pl.ds(c * CH, CH)] = rx_lo[0, pl.ds(c * CH, CH)]
        h0[pl.ds(HALO + ROWS + s * CH, CH)] = rx_hi[0, pl.ds(s * CH, CH)]

        def body0(k, carry, s=s):
            b = outward(s, k)
            cat, agg, pre, sig, act, xhat, inv, nxt = forward(0, b, h0)
            rows = pl.ds(b * BLK, RB * BLK)
            agg0[rows, :] = agg
            pre0[rows, :] = pre
            act0[rows, :] = act
            xh0[rows, :] = xhat
            inv0[rows, :] = inv
            h1[pl.ds(HALO + b, RB)] = nxt.reshape(RB, BLK, BLK)
            return carry

        lax.fori_loop(0, 2 * CH // RB, body0, 0, unroll=2)
        for late in (s,) if s < EARLY else range(NCH - 1, EARLY - 1, -1) if s == NCH - 1 else ():
            c = NCH - 1 - late
            hold(to_left(1, c, h1.at[pl.ds(HALO + c * CH, CH)]))
            hold(to_right(1, late, h1.at[pl.ds(HALO + HALO + late * CH, CH)]))
        if s < EARLY:
            release()
    first = release()
    second = release()

    get_cot.wait()
    for s in range(NCH):
        c = NCH - 1 - s
        if s == 0:
            release(first)
        wait_low(1, c)
        wait_high(1, s)
        h1[pl.ds(c * CH, CH)] = rx_lo[1, pl.ds(c * CH, CH)]
        h1[pl.ds(HALO + ROWS + s * CH, CH)] = rx_hi[1, pl.ds(s * CH, CH)]

        def body1(k, carry, s=s):
            b = outward(s, k)
            cat, agg, pre, sig, act, xhat, inv, nxt = forward(1, b, h1)
            h2[pl.ds(b, RB)] = nxt.reshape(RB, BLK, BLK)
            g = cot[pl.ds(b, RB)].reshape(RB * BLK, BLK).astype(F32)
            backward(1, b, g, cat, pre, sig, act, xhat, inv)
            return carry

        lax.fori_loop(0, 2 * CH // RB, body1, 0, unroll=2)

    def chain(seg, at, prev, value):
        seg[at] = value + jnp.where(prev >= 0, seg[jnp.maximum(prev, 0)], 0.0)

    def reach(s):
        def body(k, carry):
            t = s * CH + k
            chain(seg_a, t, tab[PREV_A + t], dot_tn(tiles[t, 1], gagg[t]))
            i = ROWS - 1 - t
            chain(seg_b, t, tab[PREV_B + t], dot_tn(tiles[i, 2], gagg[i]))
            return carry

        lax.fori_loop(0, CH, body, 0, unroll=4)

    def pick(seg, last):
        return jnp.where(last >= 0, seg[jnp.maximum(last, 0)], 0.0)

    def pack_low(y, c):
        def body(k, carry):
            out_lo[y, c * CH + k] = pick(seg_a, tab[LAST_A + c * CH + k]).astype(BF16)
            return carry

        lax.fori_loop(0, CH, body, 0, unroll=4)
        hold(to_left(2 + y, c, out_lo.at[y, pl.ds(c * CH, CH)]))

    def pack_high(y, c):
        def body(k, carry):
            out_hi[y, c * CH + k] = pick(seg_b, tab[LAST_B + HALO + c * CH + k]).astype(BF16)
            return carry

        lax.fori_loop(0, CH, body, 0, unroll=4)
        hold(to_right(2 + y, c, out_hi.at[y, pl.ds(c * CH, CH)]))

    def inside():
        def body(t, carry):
            chain(seg_c, t, tab[PREV_C + t], dot_tn(tiles[t, 2], gagg[t]))
            return carry

        lax.fori_loop(0, HALO, body, 0, unroll=16)

        def body2(t, carry):
            i = ROWS - 1 - t
            chain(seg_c, HALO + t, tab[PREV_C + HALO + t], dot_tn(tiles[i, 1], gagg[i]))
            return carry

        lax.fori_loop(0, HALO, body2, 0, unroll=16)

        def body3(j, carry):
            gacc[j] += (
                dot_tn(tiles[j, 0], gagg[j]) + pick(seg_c, tab[LAST_C + j]) + pick(seg_a, tab[LAST_A + HALO + j])
            )
            i = HALO + j
            gacc[i] += dot_tn(tiles[i, 0], gagg[i]) + pick(seg_c, tab[LAST_C + i]) + pick(seg_b, tab[LAST_B + j])
            return carry

        lax.fori_loop(0, HALO, body3, 0, unroll=16)

    def line_copy(layer, d):
        peer = lax.rem(line + d, LINE)
        return pltpu.make_async_remote_copy(
            src_ref=s1.at[layer, peer], dst_ref=r1.at[layer, d - 1], send_sem=s1_sem.at[layer, d - 1],
            recv_sem=r1_sem.at[layer, d - 1], device_id=on_line(peer), device_id_type=MESH,
        )

    def plane_copy(layer, d):
        return pltpu.make_async_remote_copy(
            src_ref=s2.at[layer], dst_ref=r2.at[layer, plane], send_sem=s2_sem.at[layer, d - 1],
            recv_sem=r2_sem.at[layer, d - 1], device_id=on_plane(lax.rem(plane + d, XZ)), device_id_type=MESH,
        )

    def gather_copy(layer, d):
        return pltpu.make_async_remote_copy(
            src_ref=s3.at[layer], dst_ref=r3.at[layer, line], send_sem=s3_sem.at[layer, d - 1],
            recv_sem=r3_sem.at[layer, d - 1], device_id=on_line(lax.rem(line + d, LINE)), device_id_type=MESH,
        )

    def reduce_line_start(layer):
        for p in range(LINE):
            s1[layer, p, pl.ds(0, WROWS), :] = acc_w[layer, pl.ds(p * WROWS, WROWS), :].astype(BF16)
            s1[layer, p, pl.ds(WROWS, 16), :] = acc_s[layer].astype(BF16)
        for d in range(1, LINE):
            line_copy(layer, d).start()

    def reduce_plane_start(layer):
        for d in range(1, LINE):
            line_copy(layer, d).wait()
        summed = s1[layer, line].astype(F32)
        for d in range(1, LINE):
            summed += r1[layer, d - 1].astype(F32)
        s2[layer] = summed.astype(BF16)
        r2[layer, plane] = summed.astype(BF16)
        for d in range(1, XZ):
            plane_copy(layer, d).start()

    def gather_start(layer):
        for d in range(1, XZ):
            plane_copy(layer, d).wait()
        summed = r2[layer, 0].astype(F32)
        for p in range(1, XZ):
            summed += r2[layer, p].astype(F32)
        summed = (summed * scale).astype(BF16)
        s3[layer] = summed
        r3[layer, line] = summed
        for d in range(1, LINE):
            gather_copy(layer, d).start()

    def finish(layer):
        for d in range(1, LINE):
            gather_copy(layer, d).wait()
        for p in range(LINE):
            piece = r3[layer, p, pl.ds(0, WROWS), :].astype(F32)
            lo, hi = p * WROWS, (p + 1) * WROWS
            cut = min(max(256 - lo, 0), WROWS)
            if cut > 0:
                out_win[layer, pl.ds(lo, cut), :] = piece[:cut]
            if cut < WROWS:
                out_wout[layer, pl.ds(lo + cut - 256, WROWS - cut), :] = piece[cut:]
        small = r3[layer, 0, pl.ds(WROWS, 16), :].astype(F32)
        out_bias[pl.ds(layer, 1), :] = small[:1]
        out_gain[pl.ds(layer, 1), :] = small[1:2]

    for s in range(NCH):
        reach(s)
    for s in range(NCH):
        pack_low(0, NCH - 1 - s)
        pack_high(0, s)
        if s < 2:
            ahead = (*ahead, release()) if s else (release(),)
    reduce_line_start(1)
    inside()
    release(ahead[0])

    for s in range(NCH):
        c = NCH - 1 - s
        if s == 0:
            release(ahead[1])
        wait_low(2, s)
        wait_high(2, c)

        def body2(k, carry, s=s):
            b = inward(s, k)
            rows = pl.ds(b * BLK, RB * BLK)
            low = b < HALO
            at_lo = jnp.where(low, b, s * CH)
            at_hi = jnp.where(low, (NCH - 1 - s) * CH, b - HALO)
            come = jnp.where(low, rx_lo[2, pl.ds(at_lo, RB)], rx_hi[2, pl.ds(at_hi, RB)])
            g = (gacc[pl.ds(b, RB)] + come.astype(F32)).reshape(RB * BLK, BLK)
            cat = jnp.concatenate([h0[pl.ds(HALO + b, RB)].reshape(RB * BLK, BLK), agg0[rows, :]], axis=1)
            pre = pre0[rows, :]
            sig = 0.5 * jnp.tanh(0.5 * pre) + 0.5
            backward(0, b, g, cat, pre, sig, act0[rows, :], xh0[rows, :], inv0[rows, :])
            return carry

        lax.fori_loop(0, 2 * CH // RB, body2, 0, unroll=2)
        reach(s)
        if s < EARLY_BACK:
            pack_low(1, s)
            pack_high(1, c)
            release()
        if s == 2:
            reduce_plane_start(1)
    reduce_line_start(0)
    for s in range(EARLY_BACK, NCH):
        pack_low(1, s)
        pack_high(1, NCH - 1 - s)
        if s < EARLY_BACK + 2:
            ahead = (*ahead, release()) if s > EARLY_BACK else (release(),)
    gather_start(1)
    inside()
    reduce_plane_start(0)
    release(ahead[0])
    while held:
        ahead = (ahead[1], release(ahead[1]))
    finish(1)

    for s in range(NCH):
        c = NCH - 1 - s
        wait_low(3, c)
        wait_high(3, s)
        for b, rx, at in ((c * CH, rx_lo, c * CH), (HALO + s * CH, rx_hi, s * CH)):
            for k in range(CH):
                gacc[b + k] += rx[3, at + k].astype(F32)
        if s == 1:
            gather_start(0)
    finish(0)
    for copy in sent:
        copy.wait_send()


def publish_kernel(*refs):
    sem = refs[12]
    copies = [pltpu.make_async_copy(refs[k], refs[6 + k], sem.at[k]) for k in range(6)]
    for copy in copies:
        copy.start()
    for copy in copies:
        copy.wait()


def per_device(feats, tile_vals, tile_offs, w_in, bias_in, w_out, gain, cot):
    nodes, width = feats.shape
    total = nodes * lax.axis_size("band") * lax.axis_size("rep")
    scale = 1.0 / math.sqrt(total)
    smem = pl.BlockSpec(memory_space=pltpu.SMEM)
    vmem = pl.BlockSpec(memory_space=pltpu.VMEM)
    hbm = pl.BlockSpec(memory_space=pl.ANY)
    blocks = (ROWS, BLK, width)
    ext = (ROWS + 2 * HALO, BLK, width)
    dma = pltpu.SemaphoreType.DMA
    outs = pl.pallas_call(
        functools.partial(main_kernel, scale),
        out_shape=(
            pltpu.VMEM(blocks, BF16),
            pltpu.VMEM(blocks, F32),
            pltpu.VMEM(w_in.shape, F32),
            pltpu.VMEM(bias_in.shape, F32),
            pltpu.VMEM(w_out.shape, F32),
            pltpu.VMEM(gain.shape, F32),
        ),
        in_specs=[hbm, hbm, hbm, smem, vmem, vmem, vmem, vmem],
        out_specs=(vmem,) * 6,
        scratch_shapes=[
            pltpu.SMEM((TABLE,), jnp.int32),
            pltpu.VMEM(tile_vals.shape, BF16),
            pltpu.VMEM(ext, BF16),
            pltpu.VMEM(ext, BF16),
            pltpu.VMEM(blocks, BF16),
            pltpu.VMEM((nodes, width), BF16),
            pltpu.VMEM((nodes, width), F32),
            pltpu.VMEM((nodes, width), BF16),
            pltpu.VMEM((nodes, width), F32),
            pltpu.VMEM((nodes, 1), F32),
            pltpu.VMEM(blocks, BF16),
            pltpu.VMEM((HALO, BLK, width), F32),
            pltpu.VMEM((HALO, BLK, width), F32),
            pltpu.VMEM((ROWS, BLK, width), F32),
            pltpu.VMEM((2, HALO, BLK, width), BF16),
            pltpu.VMEM((2, HALO, BLK, width), BF16),
            pltpu.VMEM((4, HALO, BLK, width), BF16),
            pltpu.VMEM((4, HALO, BLK, width), BF16),
            pltpu.VMEM((2, 384, 128), F32),
            pltpu.VMEM((2, 16, 128), F32),
            pltpu.VMEM((2, LINE, PIECE, 128), BF16),
            pltpu.VMEM((2, LINE - 1, PIECE, 128), BF16),
            pltpu.VMEM((2, PIECE, 128), BF16),
            pltpu.VMEM((2, XZ, PIECE, 128), BF16),
            pltpu.VMEM((2, PIECE, 128), BF16),
            pltpu.VMEM((2, LINE, PIECE, 128), BF16),
            dma((3,)),
            dma((4, NCH)),
            dma((4, NCH)),
            dma((4, NCH)),
            dma((4, NCH)),
            dma((2, LINE - 1)),
            dma((2, LINE - 1)),
            dma((2, XZ - 1)),
            dma((2, XZ - 1)),
            dma((2, LINE - 1)),
            dma((2, LINE - 1)),
        ],
        compiler_params=pltpu.CompilerParams(
            collective_id=0, has_side_effects=True, vmem_limit_bytes=56 * 2**20
        ),
        cost_estimate=pl.CostEstimate(flops=4 * 10**9, bytes_accessed=9 * 10**6, transcendentals=10**6),
    )(feats.reshape(blocks), tile_vals, cot.reshape(blocks), tile_offs.T, w_in, bias_in, w_out, gain)
    outs = (outs[0].reshape(feats.shape), outs[1].reshape(feats.shape), *outs[2:])
    return pl.pallas_call(
        publish_kernel,
        out_shape=tuple(jax.ShapeDtypeStruct(o.shape, o.dtype) for o in outs),
        in_specs=[hbm] * 6,
        out_specs=(hbm,) * 6,
        scratch_shapes=[dma((6,))],
        compiler_params=pltpu.CompilerParams(vmem_limit_bytes=2**20),
    )(*outs)


def solution(mesh):
    rows = P(("band", "rep"), None)
    placed = (rows, P(("band", "rep"), None, None, None), rows, P(), P(), P(), P(), rows)
    return jax.shard_map(
        per_device,
        mesh=mesh,
        in_specs=placed,
        out_specs=(rows, rows, P(), P(), P(), P()),
        check_vma=False,
    )
```

```python
import functools
import math

import jax
import jax.numpy as jnp
from jax import lax
from jax.experimental import pallas as pl
from jax.experimental.pallas import tpu as pltpu
from jax.sharding import PartitionSpec as P

MESH = pl.DeviceIdType.MESH
HALO = 16
ROWS = 32
BLK = 128
CH = 4
NCH = HALO // CH
EARLY = 1
EARLY_BACK = 0
RB = 4
XZ = 16
LINE = 8
PIECE = 64
WROWS = 48
F32 = jnp.float32
BF16 = jnp.bfloat16

PREV_A, PREV_B, PREV_C = 0, 16, 32
LAST_A, LAST_B, LAST_C = 64, 96, 128
COLS_A, COLS_B, COLS_C = 160, 176, 192
TABLE = 224


def links(offs, tab):
    def columns(t, carry):
        i = ROWS - 1 - t
        tab[COLS_A + t] = HALO + t + offs[1, t]
        tab[COLS_B + t] = i - HALO + offs[2, i]
        tab[COLS_C + t] = t + offs[2, t]
        tab[COLS_C + HALO + t] = i + offs[1, i]
        return carry

    lax.fori_loop(0, HALO, columns, 0)
    for cols, prev, last, count in (
        (COLS_A, PREV_A, LAST_A, HALO), (COLS_B, PREV_B, LAST_B, HALO), (COLS_C, PREV_C, LAST_C, 2 * HALO)
    ):
        def find_prev(e, carry, cols=cols, prev=prev, count=count):
            col, found = tab[cols + e], jnp.int32(-1)
            for k in range(count):
                found = jnp.where((tab[cols + k] == col) & (k < e), k, found)
            tab[prev + e] = found
            return carry

        def find_last(c, carry, cols=cols, last=last, count=count):
            found = jnp.int32(-1)
            for k in range(count):
                found = jnp.where(tab[cols + k] == c, k, found)
            tab[last + c] = found
            return carry

        lax.fori_loop(0, count, find_prev, 0)
        lax.fori_loop(0, ROWS, find_last, 0)


def dot(a, b):
    return jnp.dot(a, b, preferred_element_type=F32)


def dot_nt(a, b):
    return lax.dot_general(a, b, (((1,), (1,)), ((), ())), preferred_element_type=F32)


def dot_tn(a, b):
    return lax.dot_general(a, b, (((0,), (0,)), ((), ())), preferred_element_type=F32)


def main_kernel(
    scale,
    feats, tiles_in, cot_in, offs, w_in, bias, w_out, gain,
    h2, gacc, out_win, out_bias, out_wout, out_gain,
    tab, tiles, h0, h1, cot, agg0, pre0, act0, xh0, inv0, gagg,
    seg_a, seg_b, seg_c, out_lo, out_hi, rx_lo, rx_hi, acc_w, acc_s,
    s1, r1, s2, r2, s3, r3,
    local_sem, tx_lo_sem, tx_hi_sem, rx_lo_sem, rx_hi_sem,
    s1_sem, r1_sem, s2_sem, r2_sem, s3_sem, r3_sem,
):
    band, rep = lax.axis_index("band"), lax.axis_index("rep")
    n_rep, n_band = 4, 32
    me = band * n_rep + rep
    total = n_rep * n_band

    def place(index):
        return (lax.div(index, n_rep), lax.rem(index, n_rep))

    left = place(lax.rem(me + total - 1, total))
    right = place(lax.rem(me + 1, total))
    y_hi, x, z = lax.div(band, 16), lax.rem(lax.div(band, 4), 4), lax.rem(band, 4)
    y_lo, core = lax.div(rep, 2), lax.rem(rep, 2)
    line = x * 2 + core
    plane = z * 4 + y_hi * 2 + y_lo

    def on_line(index):
        return (y_hi * 16 + lax.div(index, 2) * 4 + z, y_lo * 2 + lax.rem(index, 2))

    def on_plane(index):
        return (
            lax.rem(lax.div(index, 2), 2) * 16 + x * 4 + lax.div(index, 4),
            lax.rem(index, 2) * 2 + core,
        )

    barrier = pltpu.get_barrier_semaphore()
    for peer in (left, right):
        pl.semaphore_signal(barrier, inc=1, device_id=peer, device_id_type=MESH)
    for d in range(1, LINE):
        pl.semaphore_signal(barrier, inc=1, device_id=on_line(lax.rem(line + d, LINE)), device_id_type=MESH)
    for d in range(1, XZ):
        pl.semaphore_signal(barrier, inc=1, device_id=on_plane(lax.rem(plane + d, XZ)), device_id_type=MESH)

    get_feats = pltpu.make_async_copy(feats, h0.at[pl.ds(HALO, ROWS)], local_sem.at[0])
    get_tiles = pltpu.make_async_copy(tiles_in, tiles, local_sem.at[1])
    get_cot = pltpu.make_async_copy(cot_in, cot, local_sem.at[2])
    get_feats.start()
    get_tiles.start()
    get_cot.start()
    acc_w[...] = jnp.zeros_like(acc_w)
    acc_s[...] = jnp.zeros_like(acc_s)

    pl.semaphore_wait(barrier, 2 + LINE - 1 + XZ - 1)

    def to_left(x, c, src):
        return pltpu.make_async_remote_copy(
            src_ref=src, dst_ref=rx_hi.at[x, pl.ds(c * CH, CH)], send_sem=tx_lo_sem.at[x, c],
            recv_sem=rx_hi_sem.at[x, c], device_id=left, device_id_type=MESH,
        )

    def to_right(x, c, src):
        return pltpu.make_async_remote_copy(
            src_ref=src, dst_ref=rx_lo.at[x, pl.ds(c * CH, CH)], send_sem=tx_hi_sem.at[x, c],
            recv_sem=rx_lo_sem.at[x, c], device_id=right, device_id_type=MESH,
        )

    sent = []

    def go(copy):
        copy.start()
        sent.append(copy)
        return copy

    held = []

    def hold(copy):
        held.append(copy)

    def release(before=()):
        for copy in before:
            copy.wait_send()
            sent[:] = [k for k in sent if k is not copy]
        for copy in (held.pop(0), held.pop(0)):
            go(copy)
        return tuple(sent[-2:])

    def wait_low(x, c):
        to_right(x, c, rx_lo.at[x, pl.ds(c * CH, CH)]).wait_recv()

    def wait_high(x, c):
        to_left(x, c, rx_hi.at[x, pl.ds(c * CH, CH)]).wait_recv()

    for s in range(NCH):
        c = NCH - 1 - s
        go(to_left(0, s, feats.at[pl.ds(s * CH, CH)]))
        go(to_right(0, c, feats.at[pl.ds(HALO + c * CH, CH)]))
    links(offs, tab)
    get_feats.wait()
    get_tiles.wait()

    def forward(layer, b, ext):
        own = ext[pl.ds(HALO + b, RB)]
        sums = []
        for r in range(RB):
            tile = tiles[b + r]
            lhs = jnp.concatenate([tile[0], tile[1]], axis=1)
            rhs = jnp.concatenate([own[r], ext[HALO + b + r + offs[1, b + r]]], axis=0)
            sums.append((dot(lhs, rhs) + dot(tile[2], ext[HALO + b + r + offs[2, b + r]])).astype(BF16))
        own = own.reshape(RB * BLK, BLK)
        agg = jnp.concatenate(sums, axis=0)
        cat = jnp.concatenate([own, agg], axis=1)
        pre = dot(cat, w_in[layer]) + bias[pl.ds(layer, 1), :]
        sig = 0.5 * jnp.tanh(0.5 * pre) + 0.5
        act = (pre * sig).astype(BF16)
        mix = dot(act, w_out[layer])
        cen = mix - jnp.mean(mix, axis=1, keepdims=True)
        inv = lax.rsqrt(jnp.mean(cen * cen, axis=1, keepdims=True) + 1e-05)
        xhat = cen * inv
        nxt = (own.astype(F32) + xhat * gain[pl.ds(layer, 1), :]).astype(BF16)
        return cat, agg, pre, sig, act, xhat, inv, nxt

    def backward(layer, b, g, cat, pre, sig, act, xhat, inv):
        gg = jnp.sum(g * xhat, axis=0, keepdims=True)
        gx = g * gain[pl.ds(layer, 1), :]
        gmix = inv * (
            gx - jnp.mean(gx, axis=1, keepdims=True) - xhat * jnp.mean(gx * xhat, axis=1, keepdims=True)
        )
        gmix_b = gmix.astype(BF16)
        gact = dot_nt(gmix_b, w_out[layer])
        gpre = gact * sig * (1.0 + pre * (1.0 - sig))
        gb = jnp.sum(gpre, axis=0, keepdims=True)
        gpre_b = gpre.astype(BF16)
        acc_w[layer, pl.ds(0, 256), :] += dot_tn(cat, gpre_b)
        acc_w[layer, pl.ds(256, 128), :] += dot_tn(act, gmix_b)
        acc_s[layer, pl.ds(0, 1), :] += gb
        acc_s[layer, pl.ds(1, 1), :] += gg
        gcat = dot_nt(gpre_b, w_in[layer])
        gacc[pl.ds(b, RB)] = (g + gcat[:, :BLK]).reshape(RB, BLK, BLK)
        gagg[pl.ds(b, RB)] = gcat[:, BLK:].astype(BF16).reshape(RB, BLK, BLK)

    def outward(s, k):
        per = CH // RB
        low = (NCH - 1 - s) * CH + k * RB
        high = HALO + s * CH + (k - per) * RB
        return jnp.where(k < per, low, high)

    def inward(s, k):
        per = CH // RB
        low = s * CH + k * RB
        high = (2 * NCH - 1 - s) * CH + (k - per) * RB
        return jnp.where(k < per, low, high)

    for s in range(NCH):
        c = NCH - 1 - s
        wait_low(0, c)
        wait_high(0, s)
        h0[pl.ds(c * CH, CH)] = rx_lo[0, pl.ds(c * CH, CH)]
        h0[pl.ds(HALO + ROWS + s * CH, CH)] = rx_hi[0, pl.ds(s * CH, CH)]

        def body0(k, carry, s=s):
            b = outward(s, k)
            cat, agg, pre, sig, act, xhat, inv, nxt = forward(0, b, h0)
            rows = pl.ds(b * BLK, RB * BLK)
            agg0[rows, :] = agg
            pre0[rows, :] = pre
            act0[rows, :] = act
            xh0[rows, :] = xhat
            inv0[rows, :] = inv
            h1[pl.ds(HALO + b, RB)] = nxt.reshape(RB, BLK, BLK)
            return carry

        lax.fori_loop(0, 2 * CH // RB, body0, 0, unroll=2)
        for late in (s,) if s < EARLY else range(NCH - 1, EARLY - 1, -1) if s == NCH - 1 else ():
            c = NCH - 1 - late
            hold(to_left(1, c, h1.at[pl.ds(HALO + c * CH, CH)]))
            hold(to_right(1, late, h1.at[pl.ds(HALO + HALO + late * CH, CH)]))
        if s < EARLY:
            release()
    first = release()
    second = release()

    get_cot.wait()
    for s in range(NCH):
        c = NCH - 1 - s
        if s == 0:
            release(first)
        wait_low(1, c)
        wait_high(1, s)
        h1[pl.ds(c * CH, CH)] = rx_lo[1, pl.ds(c * CH, CH)]
        h1[pl.ds(HALO + ROWS + s * CH, CH)] = rx_hi[1, pl.ds(s * CH, CH)]

        def body1(k, carry, s=s):
            b = outward(s, k)
            cat, agg, pre, sig, act, xhat, inv, nxt = forward(1, b, h1)
            h2[pl.ds(b, RB)] = nxt.reshape(RB, BLK, BLK)
            g = cot[pl.ds(b, RB)].reshape(RB * BLK, BLK).astype(F32)
            backward(1, b, g, cat, pre, sig, act, xhat, inv)
            return carry

        lax.fori_loop(0, 2 * CH // RB, body1, 0, unroll=2)

    def chain(seg, at, prev, value):
        seg[at] = value + jnp.where(prev >= 0, seg[jnp.maximum(prev, 0)], 0.0)

    def reach(s):
        def body(k, carry):
            t = s * CH + k
            chain(seg_a, t, tab[PREV_A + t], dot_tn(tiles[t, 1], gagg[t]))
            i = ROWS - 1 - t
            chain(seg_b, t, tab[PREV_B + t], dot_tn(tiles[i, 2], gagg[i]))
            return carry

        lax.fori_loop(0, CH, body, 0, unroll=4)

    def pick(seg, last):
        return jnp.where(last >= 0, seg[jnp.maximum(last, 0)], 0.0)

    def pack_low(y, c):
        def body(k, carry):
            out_lo[y, c * CH + k] = pick(seg_a, tab[LAST_A + c * CH + k]).astype(BF16)
            return carry

        lax.fori_loop(0, CH, body, 0, unroll=4)
        hold(to_left(2 + y, c, out_lo.at[y, pl.ds(c * CH, CH)]))

    def pack_high(y, c):
        def body(k, carry):
            out_hi[y, c * CH + k] = pick(seg_b, tab[LAST_B + HALO + c * CH + k]).astype(BF16)
            return carry

        lax.fori_loop(0, CH, body, 0, unroll=4)
        hold(to_right(2 + y, c, out_hi.at[y, pl.ds(c * CH, CH)]))

    def inside(between=None):
        def body(t, carry):
            chain(seg_c, t, tab[PREV_C + t], dot_tn(tiles[t, 2], gagg[t]))
            return carry

        lax.fori_loop(0, HALO, body, 0, unroll=16)

        def body2(t, carry):
            i = ROWS - 1 - t
            chain(seg_c, HALO + t, tab[PREV_C + HALO + t], dot_tn(tiles[i, 1], gagg[i]))
            return carry

        lax.fori_loop(0, HALO, body2, 0, unroll=16)

        if between is not None:
            between()

        def body3(j, carry):
            gacc[j] += (
                dot_tn(tiles[j, 0], gagg[j]) + pick(seg_c, tab[LAST_C + j]) + pick(seg_a, tab[LAST_A + HALO + j])
            )
            i = HALO + j
            gacc[i] += dot_tn(tiles[i, 0], gagg[i]) + pick(seg_c, tab[LAST_C + i]) + pick(seg_b, tab[LAST_B + j])
            return carry

        lax.fori_loop(0, HALO, body3, 0, unroll=16)

    def line_copy(layer, d):
        peer = lax.rem(line + d, LINE)
        return pltpu.make_async_remote_copy(
            src_ref=s1.at[layer, peer], dst_ref=r1.at[layer, d - 1], send_sem=s1_sem.at[layer, d - 1],
            recv_sem=r1_sem.at[layer, d - 1], device_id=on_line(peer), device_id_type=MESH,
        )

    def plane_copy(layer, d):
        return pltpu.make_async_remote_copy(
            src_ref=s2.at[layer], dst_ref=r2.at[layer, plane], send_sem=s2_sem.at[layer, d - 1],
            recv_sem=r2_sem.at[layer, d - 1], device_id=on_plane(lax.rem(plane + d, XZ)), device_id_type=MESH,
        )

    def gather_copy(layer, d):
        return pltpu.make_async_remote_copy(
            src_ref=s3.at[layer], dst_ref=r3.at[layer, line], send_sem=s3_sem.at[layer, d - 1],
            recv_sem=r3_sem.at[layer, d - 1], device_id=on_line(lax.rem(line + d, LINE)), device_id_type=MESH,
        )

    def reduce_line_start(layer):
        for p in range(LINE):
            s1[layer, p, pl.ds(0, WROWS), :] = acc_w[layer, pl.ds(p * WROWS, WROWS), :].astype(BF16)
            s1[layer, p, pl.ds(WROWS, 16), :] = acc_s[layer].astype(BF16)
        for d in range(1, LINE):
            line_copy(layer, d).start()

    def reduce_plane_start(layer):
        for d in range(1, LINE):
            line_copy(layer, d).wait()
        summed = s1[layer, line].astype(F32)
        for d in range(1, LINE):
            summed += r1[layer, d - 1].astype(F32)
        s2[layer] = summed.astype(BF16)
        r2[layer, plane] = summed.astype(BF16)
        for d in range(1, XZ):
            plane_copy(layer, d).start()

    def gather_start(layer):
        for d in range(1, XZ):
            plane_copy(layer, d).wait()
        summed = r2[layer, 0].astype(F32)
        for p in range(1, XZ):
            summed += r2[layer, p].astype(F32)
        summed = (summed * scale).astype(BF16)
        s3[layer] = summed
        r3[layer, line] = summed
        for d in range(1, LINE):
            gather_copy(layer, d).start()

    def finish(layer):
        for d in range(1, LINE):
            gather_copy(layer, d).wait()
        for p in range(LINE):
            piece = r3[layer, p, pl.ds(0, WROWS), :].astype(F32)
            lo, hi = p * WROWS, (p + 1) * WROWS
            cut = min(max(256 - lo, 0), WROWS)
            if cut > 0:
                out_win[layer, pl.ds(lo, cut), :] = piece[:cut]
            if cut < WROWS:
                out_wout[layer, pl.ds(lo + cut - 256, WROWS - cut), :] = piece[cut:]
        small = r3[layer, 0, pl.ds(WROWS, 16), :].astype(F32)
        out_bias[pl.ds(layer, 1), :] = small[:1]
        out_gain[pl.ds(layer, 1), :] = small[1:2]

    for s in range(NCH):
        reach(s)
    for s in range(NCH):
        pack_low(0, NCH - 1 - s)
        pack_high(0, s)
        if s < 2:
            ahead = (*ahead, release()) if s else (release(),)
    reduce_line_start(1)
    inside()
    release(ahead[0])

    for s in range(NCH):
        c = NCH - 1 - s
        if s == 0:
            release(ahead[1])
        wait_low(2, s)
        wait_high(2, c)

        def body2(k, carry, s=s):
            b = inward(s, k)
            rows = pl.ds(b * BLK, RB * BLK)
            low = b < HALO
            at_lo = jnp.where(low, b, s * CH)
            at_hi = jnp.where(low, (NCH - 1 - s) * CH, b - HALO)
            come = jnp.where(low, rx_lo[2, pl.ds(at_lo, RB)], rx_hi[2, pl.ds(at_hi, RB)])
            g = (gacc[pl.ds(b, RB)] + come.astype(F32)).reshape(RB * BLK, BLK)
            cat = jnp.concatenate([h0[pl.ds(HALO + b, RB)].reshape(RB * BLK, BLK), agg0[rows, :]], axis=1)
            pre = pre0[rows, :]
            sig = 0.5 * jnp.tanh(0.5 * pre) + 0.5
            backward(0, b, g, cat, pre, sig, act0[rows, :], xh0[rows, :], inv0[rows, :])
            return carry

        lax.fori_loop(0, 2 * CH // RB, body2, 0, unroll=2)
        if s == NCH - 1:
            reduce_line_start(0)
        reach(s)
        if s < EARLY_BACK:
            pack_low(1, s)
            pack_high(1, c)
            release()
        if s == 2:
            reduce_plane_start(1)
    for s in range(EARLY_BACK, NCH):
        pack_low(1, s)
        pack_high(1, NCH - 1 - s)
        if s < EARLY_BACK + 2:
            ahead = (*ahead, release()) if s > EARLY_BACK else (release(),)
    gather_start(1)
    inside(functools.partial(reduce_plane_start, 0))
    release(ahead[0])
    while held:
        ahead = (ahead[1], release(ahead[1]))
    finish(1)

    for s in range(NCH):
        c = NCH - 1 - s
        wait_low(3, c)
        wait_high(3, s)
        for b, rx, at in ((c * CH, rx_lo, c * CH), (HALO + s * CH, rx_hi, s * CH)):
            for k in range(CH):
                gacc[b + k] += rx[3, at + k].astype(F32)
        if s == 1:
            gather_start(0)
    finish(0)
    for copy in sent:
        copy.wait_send()


def publish_kernel(*refs):
    sem = refs[12]
    copies = [pltpu.make_async_copy(refs[k], refs[6 + k], sem.at[k]) for k in range(6)]
    for copy in copies:
        copy.start()
    for copy in copies:
        copy.wait()


def per_device(feats, tile_vals, tile_offs, w_in, bias_in, w_out, gain, cot):
    nodes, width = feats.shape
    total = nodes * lax.axis_size("band") * lax.axis_size("rep")
    scale = 1.0 / math.sqrt(total)
    smem = pl.BlockSpec(memory_space=pltpu.SMEM)
    vmem = pl.BlockSpec(memory_space=pltpu.VMEM)
    hbm = pl.BlockSpec(memory_space=pl.ANY)
    blocks = (ROWS, BLK, width)
    ext = (ROWS + 2 * HALO, BLK, width)
    dma = pltpu.SemaphoreType.DMA
    outs = pl.pallas_call(
        functools.partial(main_kernel, scale),
        out_shape=(
            pltpu.VMEM(blocks, BF16),
            pltpu.VMEM(blocks, F32),
            pltpu.VMEM(w_in.shape, F32),
            pltpu.VMEM(bias_in.shape, F32),
            pltpu.VMEM(w_out.shape, F32),
            pltpu.VMEM(gain.shape, F32),
        ),
        in_specs=[hbm, hbm, hbm, smem, vmem, vmem, vmem, vmem],
        out_specs=(vmem,) * 6,
        scratch_shapes=[
            pltpu.SMEM((TABLE,), jnp.int32),
            pltpu.VMEM(tile_vals.shape, BF16),
            pltpu.VMEM(ext, BF16),
            pltpu.VMEM(ext, BF16),
            pltpu.VMEM(blocks, BF16),
            pltpu.VMEM((nodes, width), BF16),
            pltpu.VMEM((nodes, width), F32),
            pltpu.VMEM((nodes, width), BF16),
            pltpu.VMEM((nodes, width), F32),
            pltpu.VMEM((nodes, 1), F32),
            pltpu.VMEM(blocks, BF16),
            pltpu.VMEM((HALO, BLK, width), F32),
            pltpu.VMEM((HALO, BLK, width), F32),
            pltpu.VMEM((ROWS, BLK, width), F32),
            pltpu.VMEM((2, HALO, BLK, width), BF16),
            pltpu.VMEM((2, HALO, BLK, width), BF16),
            pltpu.VMEM((4, HALO, BLK, width), BF16),
            pltpu.VMEM((4, HALO, BLK, width), BF16),
            pltpu.VMEM((2, 384, 128), F32),
            pltpu.VMEM((2, 16, 128), F32),
            pltpu.VMEM((2, LINE, PIECE, 128), BF16),
            pltpu.VMEM((2, LINE - 1, PIECE, 128), BF16),
            pltpu.VMEM((2, PIECE, 128), BF16),
            pltpu.VMEM((2, XZ, PIECE, 128), BF16),
            pltpu.VMEM((2, PIECE, 128), BF16),
            pltpu.VMEM((2, LINE, PIECE, 128), BF16),
            dma((3,)),
            dma((4, NCH)),
            dma((4, NCH)),
            dma((4, NCH)),
            dma((4, NCH)),
            dma((2, LINE - 1)),
            dma((2, LINE - 1)),
            dma((2, XZ - 1)),
            dma((2, XZ - 1)),
            dma((2, LINE - 1)),
            dma((2, LINE - 1)),
        ],
        compiler_params=pltpu.CompilerParams(
            collective_id=0, has_side_effects=True, vmem_limit_bytes=56 * 2**20
        ),
        cost_estimate=pl.CostEstimate(flops=4 * 10**9, bytes_accessed=9 * 10**6, transcendentals=10**6),
    )(feats.reshape(blocks), tile_vals, cot.reshape(blocks), tile_offs.T, w_in, bias_in, w_out, gain)
    outs = (outs[0].reshape(feats.shape), outs[1].reshape(feats.shape), *outs[2:])
    return pl.pallas_call(
        publish_kernel,
        out_shape=tuple(jax.ShapeDtypeStruct(o.shape, o.dtype) for o in outs),
        in_specs=[hbm] * 6,
        out_specs=(hbm,) * 6,
        scratch_shapes=[dma((6,))],
        compiler_params=pltpu.CompilerParams(vmem_limit_bytes=2**20),
    )(*outs)


def solution(mesh):
    rows = P(("band", "rep"), None)
    placed = (rows, P(("band", "rep"), None, None, None), rows, P(), P(), P(), P(), rows)
    return jax.shard_map(
        per_device,
        mesh=mesh,
        in_specs=placed,
        out_specs=(rows, rows, P(), P(), P(), P()),
        check_vma=False,
    )
```
